256 devices in a mesh: section: 4 (over x), fsdp: 64 (over y, z, core).
Axes of the slice: x: 4, y: 4, z: 8, core: 2. Of those that a mesh axis runs over, the one named last changes fastest.
Arguments:
- enc_states: bfloat16 [64, 4, 1280], P('fsdp'), may hold values from -6 to 6
- clip_frames: int32 [64], replicated, may hold values from 2 to 4, as said below
- clip_offset: int32 [64], replicated, may hold values from 0 to 126, as said below
- ln_gain: float32 [1280], replicated, may hold values from 0.1 to 1.9
- ln_bias: float32 [1280], replicated, may hold values from -0.6 to 0.6
- w_proj: bfloat16 [1280, 8192], P(None, 'fsdp'), may hold values from -0.15625 to 0.15625
- proj_bias: float32 [8192], P('fsdp'), may hold values from -3 to 3
- text_embed: bfloat16 [64, 2, 8192], P(None, None, 'fsdp'), may hold values from -6 to 6
- norm_gain: float32 [4, 8192], P('section'), may hold values from 0.1 to 1.9
- w_gate: bfloat16 [4, 14784, 8192], P('section', 'fsdp'), may hold values from -0.0625 to 0.0625
- w_up: bfloat16 [4, 14784, 8192], P('section', 'fsdp'), may hold values from -0.0625 to 0.0625
- w_down: bfloat16 [4, 14784, 8192], P('section', 'fsdp'), may hold values from -0.046875 to 0.046875
Outputs:
- stream_out: bfloat16 [64, 2, 8192], P('section', None, 'fsdp')
The draws below stay inside these ranges and needn't reach their ends.
Inputs may be any that keep to these rules, and one draw needn't show every extreme that they name: `clip_frames`: every clip's frame count is even, and some clip has exactly 4 frames. Clip c's live rows occupy stream positions clip_offset[c] to clip_offset[c] + clip_frames[c] / 2 - 1, all inside one microbatch (positions m * 64 to (m + 1) * 64 - 1); no two clips share a position; each microbatch holds 32 clips.
All inputs are finite; a program needn't handle non-finite values.
Results may differ from the reference program's by a relative error of at most 0.015.
Values may be sent and summed in bfloat16 or wider, within the bound.
A program may use at most 64 MiB of HBM per device.

```python
import jax
import jax.numpy as jnp
from jax import lax

D = 8192
FF = 14784
DE = 1280
CLIP_ROWS = 2
MICRO = 2
TOKENS = 64
FRAMES = 4
CLIPS = 64
LAYERS = 4


def clip_layout(key):
    base = jax.random.fold_in(key, 11)
    key_rows, key_order, key_gaps = jax.random.split(base, 3)
    counts = jax.random.randint(key_rows, (CLIPS,), 1, CLIP_ROWS + 1).astype(jnp.int32)
    counts = counts.at[0].set(CLIP_ROWS)
    rest = (jax.random.permutation(key_order, CLIPS - 1) + 1).astype(jnp.int32)
    order = jnp.concatenate([rest, jnp.zeros((1,), jnp.int32)]).astype(jnp.int32)
    per_micro = CLIPS // MICRO
    slot_rows = counts[order].reshape(MICRO, per_micro)
    spare = TOKENS - jnp.sum(slot_rows, axis=1)
    weights = jax.random.randint(key_gaps, (MICRO, per_micro + 1), 1, 101).astype(jnp.int32)
    gaps = spare[:, None] * weights // jnp.sum(weights, axis=1, keepdims=True)
    gaps = gaps.at[0, 0].set(0)
    before = jnp.cumsum(slot_rows, axis=1) - slot_rows
    starts = jnp.cumsum(gaps[:, :per_micro], axis=1) + before
    starts = starts.at[MICRO - 1, per_micro - 1].set(TOKENS - CLIP_ROWS)
    starts = starts + (jnp.arange(MICRO, dtype=jnp.int32) * TOKENS)[:, None]
    offsets = jnp.zeros((CLIPS,), jnp.int32).at[order].set(starts.reshape(-1).astype(jnp.int32))
    return (2 * counts, offsets)


def draw_clip_frames(key, part):
    frames, offsets = clip_layout(key)
    return frames


def draw_clip_offset(key, part):
    frames, offsets = clip_layout(key)
    return offsets


def level_of(stream_key, shape, shards, smallest, largest):
    loudness = 1.0
    for dim, shards_of in shards:
        heights = jax.random.uniform(jax.random.fold_in(jax.random.fold_in(stream_key, 6), dim), (shards_of,), jnp.float32, smallest / len(shards), largest / len(shards))
        loudness = loudness * jnp.repeat(jnp.exp(heights), shape[dim] // shards_of).reshape((-1,) + (1,) * (len(shape) - 1 - dim))
    return loudness


def scatter_about(rng, shape, deviation, most, cuts=(), kind=jnp.bfloat16):
    result = deviation * jax.random.normal(rng, shape, jnp.float32)
    if cuts:
        result = result * level_of(rng, shape, cuts, -0.22, 0.18)
    return jnp.clip(result, -most, most).astype(kind)


def setup_inputs(seed: int = 0) -> dict:
    key_list = jax.random.split(jax.random.key(seed), 13)
    return {
        "enc_states": scatter_about(key_list[0], (CLIPS, FRAMES, DE), 1.0, 6.0, ((0, 64),)),
        "clip_frames": draw_clip_frames(jax.random.fold_in(key_list[12], 71), 0),
        "clip_offset": draw_clip_offset(jax.random.fold_in(key_list[12], 71), 0),
        "ln_gain": jnp.clip(1.0 + 0.18 * jax.random.normal(key_list[3], (DE,), jnp.float32), 0.1, 1.9),
        "ln_bias": jnp.clip(jax.random.uniform(key_list[4], (DE,), jnp.float32, -0.6, 0.6), -0.6, 0.6),
        "w_proj": scatter_about(key_list[5], (DE, D), DE ** -0.5, 0.15625, ((1, 64),)),
        "proj_bias": scatter_about(key_list[6], (D,), 0.5, 3.0, ((0, 64),), jnp.float32),
        "text_embed": scatter_about(key_list[7], (TOKENS, MICRO, D), 1.0, 6.0, ((2, 64),)),
        "norm_gain": jnp.clip(1.0 + 0.18 * jax.random.normal(key_list[8], (LAYERS, D), jnp.float32), 0.1, 1.9),
        "w_gate": scatter_about(key_list[9], (LAYERS, FF, D), D ** -0.5, 0.0625, ((0, 4), (1, 64))),
        "w_up": scatter_about(key_list[10], (LAYERS, FF, D), D ** -0.5, 0.0625, ((0, 4), (1, 64))),
        "w_down": scatter_about(key_list[11], (LAYERS, FF, D), FF ** -0.5, 0.046875, ((0, 4), (1, 64))),
    }


def rms_scaled(stream, gain):
    values = stream.astype(jnp.float32)
    scale = lax.rsqrt(lax.optimization_barrier(jnp.mean(values * values, axis=-1, keepdims=True)) + 1e-06)
    return (values * scale * gain.astype(jnp.float32)).astype(jnp.bfloat16)

def reference(enc_states, clip_frames, clip_offset, ln_gain, ln_bias, w_proj, proj_bias, text_embed, norm_gain, w_gate, w_up, w_down):
    pairs = enc_states.astype(jnp.float32).reshape(CLIPS, CLIP_ROWS, 2, DE)
    pooled = 0.5 * (pairs[:, :, 0] + pairs[:, :, 1])
    centre = lax.optimization_barrier(jnp.mean(pooled, axis=-1, keepdims=True))
    centred = pooled - centre
    spread = lax.optimization_barrier(jnp.mean(centred * centred, axis=-1, keepdims=True))
    audio_ln = (centred * lax.rsqrt(spread + 1e-05) * ln_gain.astype(jnp.float32) + ln_bias.astype(jnp.float32)).astype(jnp.bfloat16)
    audio_ln = audio_ln.reshape(CLIPS * CLIP_ROWS, DE)
    projected = (jnp.dot(audio_ln, w_proj, preferred_element_type=jnp.float32) + proj_bias.astype(jnp.float32)).astype(jnp.bfloat16)
    within = jnp.arange(CLIP_ROWS, dtype=jnp.int32)
    live = within[None, :] * 2 < clip_frames[:, None]
    spot = clip_offset[:, None] + within[None, :]
    target = jnp.where(live, spot % TOKENS * MICRO + spot // TOKENS, TOKENS * MICRO).astype(jnp.int32).reshape(-1)
    flags = jnp.zeros((TOKENS * MICRO,), jnp.int32).at[target].set(1, mode='drop')
    placed = jnp.zeros((TOKENS * MICRO, D), jnp.bfloat16).at[target].set(projected, mode='drop')
    stream = jnp.where(flags[:, None] == 1, placed, text_embed.reshape(TOKENS * MICRO, D))
    dims = (((1,), (1,)), ((), ()))
    for layer in range(LAYERS):
        normed = rms_scaled(stream, norm_gain[layer])
        gate = lax.dot_general(normed, w_gate[layer], dims, preferred_element_type=jnp.float32)
        up = lax.dot_general(normed, w_up[layer], dims, preferred_element_type=jnp.float32)
        hidden = (jax.nn.silu(gate) * up).astype(jnp.bfloat16)
        branch = jnp.dot(hidden, w_down[layer], preferred_element_type=jnp.float32)
        stream = (stream.astype(jnp.float32) + branch).astype(jnp.bfloat16)
    return stream.reshape(TOKENS, MICRO, D)
```

```python
import functools

import jax
import jax.numpy as jnp
from jax import lax
from jax.experimental import pallas as pl
from jax.experimental.pallas import tpu as pltpu
from jax.sharding import PartitionSpec as P

MESH = pl.DeviceIdType.MESH
CHUNKS = 4
STARTS = (0.0, 4.5, 9.5, 11.0, 17.0, 21.5)
INTERVAL = 6.0


def remote(src, dst, send, recv, section, place):
    return pltpu.make_async_remote_copy(
        src_ref=src,
        dst_ref=dst,
        send_sem=send,
        recv_sem=recv,
        device_id=(section, place),
        device_id_type=MESH,
    )


def kernel(
    sections,
    ny,
    nz,
    enc_ref,
    frames_ref,
    offset_ref,
    ln_gain_ref,
    ln_bias_ref,
    proj_ref,
    proj_bias_ref,
    text_ref,
    gain_ref,
    gate_hbm,
    up_hbm,
    down_hbm,
    out_ref,
    gate_w,
    up_w,
    down_w,
    small,
    audio,
    embedded,
    full,
    scaled,
    parts,
    from_core,
    by_core,
    from_y,
    by_y,
    from_z,
    passed,
    weight_sem,
    small_s,
    small_r,
    audio_y_s,
    audio_y_r,
    audio_c_s,
    audio_c_r,
    gz_s,
    gz_r,
    gy_s,
    gy_r,
    gc_s,
    gc_r,
    rc_s,
    rc_r,
    ry_s,
    ry_r,
    rz_s,
    rz_r,
    pass_s,
    pass_r,
):
    f32, bf16 = jnp.float32, jnp.bfloat16
    section = lax.axis_index("section")
    place = lax.axis_index("fsdp")
    core = place % 2
    z = (place // 2) % nz
    y = place // (2 * nz)
    chunks, rows = full.shape[0], full.shape[4]
    total = chunks * rows
    each = chunks // sections
    last = section // (sections - 1)
    enc_width = enc_ref.shape[-1]
    tiles = enc_width // 128

    def at(y_, z_, core_):
        return (y_ * nz + z_) * 2 + core_

    sibling = at(y, z, 1 - core)

    loads = [
        pltpu.make_async_copy(src.at[0], dst, weight_sem.at[i])
        for i, (src, dst) in enumerate(((gate_hbm, gate_w), (up_hbm, up_w), (down_hbm, down_w)))
    ]
    for load in loads:
        load.start()

    barrier = pltpu.get_barrier_semaphore()
    greeted = 0
    for ds in range(sections):
        for dz in range(nz):
            if ds or dz:
                pl.semaphore_signal(
                    barrier,
                    inc=1,
                    device_id=((section + ds) % sections, at(y, (z + dz) % nz, core)),
                    device_id_type=MESH,
                )
                greeted += 1
    for dy in range(1, ny):
        pl.semaphore_signal(
            barrier, inc=1, device_id=(section, at((y + dy) % ny, z, core)), device_id_type=MESH
        )
        greeted += 1
    pl.semaphore_signal(barrier, inc=1, device_id=(section, sibling), device_id_type=MESH)
    greeted += 1

    small[z] = jnp.zeros(small.shape[1:], f32)
    frames = enc_ref[0].astype(f32)
    for j in range(2):
        pooled = 0.5 * (frames[2 * j : 2 * j + 1] + frames[2 * j + 1 : 2 * j + 2])
        centred = pooled - jnp.mean(pooled, axis=-1, keepdims=True)
        spread = jnp.mean(centred * centred, axis=-1, keepdims=True)
        normed = centred * lax.rsqrt(spread + 1e-05) * ln_gain_ref[...] + ln_bias_ref[...]
        normed = normed.astype(bf16).astype(f32)
        for t in range(tiles):
            small[z, j * tiles + t : j * tiles + t + 1, :] = normed[:, t * 128 : (t + 1) * 128]
    pl.semaphore_wait(barrier, greeted)

    sends = []
    arrivals = []
    for d in range(1, nz):
        other = (z + d) % nz
        copy = remote(small.at[z], small.at[z], small_s.at[d], small_r.at[z], section, at(y, other, core))
        copy.start()
        sends.append(copy)
        arrivals.append(
            remote(small.at[other], small.at[other], small_s.at[d], small_r.at[other], section, at(y, other, core))
        )

    clips = ny * nz * 2
    row_of = lax.broadcasted_iota(jnp.int32, (clips, 2 * clips), 1)
    clip_of = lax.broadcasted_iota(jnp.int32, (clips, 2 * clips), 0)
    holds = ((row_of // (2 * nz) % ny) * nz + row_of % nz) * 2 + row_of // (2 * nz * ny)
    which = row_of // nz % 2
    spots = jnp.zeros((8, 2 * clips), f32)
    for j in range(2):
        spot = offset_ref[...] + j
        tokens = total // 2
        target = jnp.where(2 * j < frames_ref[...], spot % tokens * 2 + spot // tokens, total)
        order = jnp.where((holds == clip_of) & (which == j), 1.0, 0.0).astype(bf16)
        spread_target = jnp.broadcast_to(target.astype(f32), (8, clips)).astype(bf16)
        spots = spots + jnp.dot(spread_target, order, preferred_element_type=f32)
    slot = lax.broadcasted_iota(jnp.int32, (total, 2 * clips), 0).astype(f32)
    chosen = jnp.where(slot == spots[0:1], 1.0, 0.0)
    taken = jnp.sum(chosen, axis=-1, keepdims=True)
    chosen = chosen.astype(bf16)

    for copy in arrivals:
        copy.wait_recv()
    for t in range(tiles):
        pair = jnp.concatenate([small[:, t, :], small[:, tiles + t, :]], axis=0)
        audio[core, y, :, t * 128 : (t + 1) * 128] = pair.astype(bf16)
    arrivals = []
    for d in range(1, ny):
        other = (y + d) % ny
        copy = remote(
            audio.at[core, y], audio.at[core, y], audio_y_s.at[d], audio_y_r.at[y], section, at(other, z, core)
        )
        copy.start()
        sends.append(copy)
        arrivals.append(
            remote(
                audio.at[core, other],
                audio.at[core, other],
                audio_y_s.at[d],
                audio_y_r.at[other],
                section,
                at(other, z, core),
            )
        )
    for copy in arrivals:
        copy.wait_recv()
    copy = remote(audio.at[core], audio.at[core], audio_c_s.at[0], audio_c_r.at[0], section, sibling)
    copy.start()
    sends.append(copy)
    remote(audio.at[1 - core], audio.at[1 - core], audio_c_s.at[0], audio_c_r.at[0], section, sibling).wait_recv()
    gathered = audio[...].reshape(2 * clips, enc_width)
    projected = jnp.dot(gathered, proj_ref[...], preferred_element_type=f32) + proj_bias_ref[...]
    placed = jnp.dot(chosen, projected.astype(bf16), preferred_element_type=f32)
    embedded[...] = jnp.where(taken > 0.0, placed, text_ref[...].astype(f32)).astype(bf16)

    hidden_units = gate_w.shape[0]
    dims = (((1,), (1,)), ((), ()))

    def total_of(k):
        value = passed[k].astype(f32)
        for other in range(nz):
            value = value + from_z[k, other].astype(f32)
        return value.astype(bf16)

    def wait_stream(k):
        for other in range(nz):
            remote(
                from_z.at[k, other], from_z.at[k, other], rz_s.at[0, 0], rz_r.at[k, other], section, sibling
            ).wait_recv()
        remote(passed.at[k], passed.at[k], pass_s.at[0], pass_r.at[k], section, sibling).wait_recv()

    def begin(k):
        own = full.at[k, core, y, z]

        @pl.when(section == 0)
        def _():
            own[...] = embedded[k * rows : (k + 1) * rows, :]

        @pl.when(section > 0)
        def _():
            wait_stream(k)
            own[...] = total_of(k)

        for d in range(1, nz):
            remote(own, own, gz_s.at[k, d], gz_r.at[k, z], section, at(y, (z + d) % nz, core)).start()
        to, slot_of = onward(k)
        if k // each == sections - 1:

            @pl.when(section == sections - 1)
            def _():
                pltpu.make_async_copy(own, passed.at[slot_of], pass_r.at[slot_of]).start()

            @pl.when(section < sections - 1)
            def _():
                remote(own, passed.at[slot_of], pass_s.at[k], pass_r.at[slot_of], to, place).start()

        else:
            remote(own, passed.at[slot_of], pass_s.at[k], pass_r.at[slot_of], to, place).start()

    def onward(k):
        to = (section + 1) * (1 - last) + (k // each) * last
        slot_of = k + last * (chunks + k % each - k)
        return to, slot_of

    def gather_y(k):
        for d in range(1, nz):
            other = (z + d) % nz
            block = full.at[k, core, y, other]
            remote(block, block, gz_s.at[k, d], gz_r.at[k, other], section, sibling).wait_recv()
        block = full.at[k, core, y]
        for d in range(1, ny):
            remote(block, block, gy_s.at[k, d], gy_r.at[k, y], section, at((y + d) % ny, z, core)).start()

    def gather_core(k):
        for d in range(1, ny):
            other = (y + d) % ny
            block = full.at[k, core, other]
            remote(block, block, gy_s.at[k, d], gy_r.at[k, other], section, sibling).wait_recv()
        block = full.at[k, core]
        remote(block, block, gc_s.at[k], gc_r.at[k], section, sibling).start()

    def compute(k):
        block = full.at[k, 1 - core]
        remote(block, block, gc_s.at[k], gc_r.at[k], section, sibling).wait_recv()
        if k == 0:
            for load in loads:
                load.wait()
        squares = jnp.zeros((rows, 128), f32)
        for b in range(2 * ny * nz):
            value = full[k, b % 2, b // (2 * nz), b // 2 % nz].astype(f32)
            squares = squares + value * value
            lanes = slice(b * 128, (b + 1) * 128)
            scaled[:, lanes] = (value * gain_ref[:, lanes]).astype(bf16)
        width = 2 * ny * nz * 128
        scale = lax.rsqrt(jnp.sum(squares, axis=-1, keepdims=True) / width + 1e-06)
        gate = lax.dot_general(scaled[...], gate_w[...], dims, preferred_element_type=f32) * scale
        up = lax.dot_general(scaled[...], up_w[...], dims, preferred_element_type=f32) * scale
        hidden = (gate / (1.0 + jnp.exp(-gate)) * up).astype(bf16)
        step = min(1024, width)
        for n in range(width // step):
            value = jnp.dot(hidden, down_w[:, n * step : (n + 1) * step], preferred_element_type=f32).astype(bf16)
            for i in range(step // 128):
                b = n * (step // 128) + i
                parts[k, b % 2, b // (2 * nz), b // 2 % nz] = value[:, i * 128 : (i + 1) * 128]
        remote(parts.at[k, 1 - core], from_core.at[k], rc_s.at[k], rc_r.at[k], section, sibling).start()

    def reduce_y(k):
        remote(parts.at[k, 1 - core], from_core.at[k], rc_s.at[k], rc_r.at[k], section, sibling).wait_recv()
        by_core[k] = (parts[k, core].astype(f32) + from_core[k].astype(f32)).astype(bf16)
        for d in range(1, ny):
            other = (y + d) % ny
            remote(
                by_core.at[k, other], from_y.at[k, d], ry_s.at[k, d], ry_r.at[k, d], section, at(other, z, core)
            ).start()

    def reduce_z(k):
        for d in range(1, ny):
            remote(by_core.at[k, 0], from_y.at[k, d], ry_s.at[k, d], ry_r.at[k, d], section, sibling).wait_recv()
        value = by_core[k, y].astype(f32)
        for d in range(1, ny):
            value = value + from_y[k, d].astype(f32)
        by_y[k] = value.astype(bf16)
        to, slot_of = onward(k)
        for d in range(nz):
            other = (z + d) % nz
            copy = remote(
                by_y.at[k, other], from_z.at[slot_of, z], rz_s.at[k, d], rz_r.at[slot_of, z], to, at(y, other, core)
            )
            if d == 0 and k // each == sections - 1:

                @pl.when(section == sections - 1)
                def _():
                    pltpu.make_async_copy(by_y.at[k, z], from_z.at[slot_of, z], rz_r.at[slot_of, z]).start()

                @pl.when(section < sections - 1)
                def _():
                    copy.start()

            else:
                copy.start()

    phases = (begin, gather_y, gather_core, compute, reduce_y, reduce_z)
    plan = sorted((STARTS[p] + INTERVAL * k, p, k) for p in range(len(phases)) for k in range(chunks))
    for _, p, k in plan:
        phases[p](k)

    for i in range(each):
        wait_stream(chunks + i)
        out_ref[i * rows : (i + 1) * rows, :] = total_of(chunks + i)

    for copy in sends:
        copy.wait_send()
    for k in range(chunks):
        own = full.at[k, core, y, z]
        for d in range(1, nz):
            remote(own, own, gz_s.at[k, d], gz_r.at[k, z], section, sibling).wait_send()
        block = full.at[k, core, y]
        for d in range(1, ny):
            remote(block, block, gy_s.at[k, d], gy_r.at[k, y], section, sibling).wait_send()
        block = full.at[k, core]
        remote(block, block, gc_s.at[k], gc_r.at[k], section, sibling).wait_send()
        remote(parts.at[k, 1 - core], from_core.at[k], rc_s.at[k], rc_r.at[k], section, sibling).wait_send()
        for d in range(1, ny):
            remote(
                by_core.at[k, (y + d) % ny], from_y.at[k, d], ry_s.at[k, d], ry_r.at[k, d], section, sibling
            ).wait_send()
        stays = k // each == sections - 1
        for d in range(nz):
            copy = remote(
                by_y.at[k, (z + d) % nz], from_z.at[k, z], rz_s.at[k, d], rz_r.at[k, z], section, sibling
            )
            if d == 0 and stays:
                pl.when(section < sections - 1)(copy.wait_send)
            else:
                copy.wait_send()
        copy = remote(own, passed.at[k], pass_s.at[k], pass_r.at[k], section, sibling)
        if stays:
            pl.when(section < sections - 1)(copy.wait_send)
        else:
            copy.wait_send()


def on_device(
    sections,
    ny,
    nz,
    enc_states,
    clip_frames,
    clip_offset,
    ln_gain,
    ln_bias,
    w_proj,
    proj_bias,
    text_embed,
    norm_gain,
    w_gate,
    w_up,
    w_down,
):
    tokens, micro, feat = text_embed.shape
    total = tokens * micro
    hidden_units, width = w_gate.shape[1:]
    chunks = CHUNKS
    rows = total // chunks
    each = chunks // sections
    enc_width = enc_states.shape[-1]
    small_rows = -(-2 * (enc_width // 128) // 8) * 8
    bf16, f32 = jnp.bfloat16, jnp.float32
    vmem = pl.BlockSpec(memory_space=pltpu.VMEM)
    hbm = pl.BlockSpec(memory_space=pl.ANY)
    dma = pltpu.SemaphoreType.DMA
    out = pl.pallas_call(
        functools.partial(kernel, sections, ny, nz),
        out_shape=jax.ShapeDtypeStruct((total // sections, feat), bf16),
        in_specs=[vmem] * 9 + [hbm] * 3,
        out_specs=vmem,
        scratch_shapes=[
            pltpu.VMEM((hidden_units, width), bf16),
            pltpu.VMEM((hidden_units, width), bf16),
            pltpu.VMEM((hidden_units, width), bf16),
            pltpu.VMEM((nz, small_rows, 128), f32),
            pltpu.VMEM((2, ny, 2 * nz, enc_width), bf16),
            pltpu.VMEM((total, feat), bf16),
            pltpu.VMEM((chunks, 2, ny, nz, rows, feat), bf16),
            pltpu.VMEM((rows, width), bf16),
            pltpu.VMEM((chunks, 2, ny, nz, rows, feat), bf16),
            pltpu.VMEM((chunks, ny, nz, rows, feat), bf16),
            pltpu.VMEM((chunks, ny, nz, rows, feat), bf16),
            pltpu.VMEM((chunks, ny, nz, rows, feat), bf16),
            pltpu.VMEM((chunks, nz, rows, feat), bf16),
            pltpu.VMEM((chunks + each, nz, rows, feat), bf16),
            pltpu.VMEM((chunks + each, rows, feat), bf16),
            dma((3,)),
            dma((nz,)),
            dma((nz,)),
            dma((ny,)),
            dma((ny,)),
            dma((1,)),
            dma((1,)),
            dma((chunks, nz)),
            dma((chunks, nz)),
            dma((chunks, ny)),
            dma((chunks, ny)),
            dma((chunks,)),
            dma((chunks,)),
            dma((chunks,)),
            dma((chunks,)),
            dma((chunks, ny)),
            dma((chunks, ny)),
            dma((chunks, nz)),
            dma((chunks + each, nz)),
            dma((chunks,)),
            dma((chunks + each,)),
        ],
        compiler_params=pltpu.CompilerParams(
            collective_id=0, has_side_effects=True, vmem_limit_bytes=48 * 2**20
        ),
        cost_estimate=pl.CostEstimate(
            flops=6 * total * hidden_units * width, bytes_accessed=6 * hidden_units * width, transcendentals=0
        ),
    )(
        enc_states,
        clip_frames.reshape(1, -1),
        clip_offset.reshape(1, -1),
        ln_gain.reshape(1, -1),
        ln_bias.reshape(1, -1),
        w_proj,
        proj_bias.reshape(1, -1),
        text_embed.reshape(total, feat),
        norm_gain,
        w_gate,
        w_up,
        w_down,
    )
    return out.reshape(tokens // sections, micro, feat)


def solution(mesh):
    sections, spread = mesh.shape["section"], mesh.shape["fsdp"]
    ny = 4 if spread == 64 else 2
    nz = spread // (2 * ny)
    placed = (
        P("fsdp", None, None),
        P(),
        P(),
        P(),
        P(),
        P(None, "fsdp"),
        P("fsdp"),
        P(None, None, "fsdp"),
        P("section", None),
        P("section", "fsdp", None),
        P("section", "fsdp", None),
        P("section", "fsdp", None),
    )
    return jax.shard_map(
        functools.partial(on_device, sections, ny, nz),
        mesh=mesh,
        in_specs=placed,
        out_specs=P("section", None, "fsdp"),
        check_vma=False,
    )
```

```python
import functools

import jax
import jax.numpy as jnp
from jax import lax
from jax.experimental import pallas as pl
from jax.experimental.pallas import tpu as pltpu
from jax.sharding import PartitionSpec as P

MESH = pl.DeviceIdType.MESH
CHUNKS = 4
BEGIN, PAIR, PAIR_STEP, OWN = 0.0, 2.6, 0.6, 4.7
FROM_Y, FROM_Y_STEP, FROM_CORE, FROM_CORE_STEP = 7.2, 0.4, 8.3, 0.3
DOWN, ADD_CORE, SUM_Y, SUM_Y_STEP = 9.6, 11.0, 15.0, 0.6
INTERVAL = 7.0


def near_first(count):
    return sorted(range(count), key=lambda d: (min(d, count - d), d))


def remote(src, dst, send, recv, section, place):
    return pltpu.make_async_remote_copy(
        src_ref=src,
        dst_ref=dst,
        send_sem=send,
        recv_sem=recv,
        device_id=(section, place),
        device_id_type=MESH,
    )


def kernel(
    sections,
    ny,
    nz,
    enc_hbm,
    frames_hbm,
    offset_hbm,
    ln_gain_hbm,
    ln_bias_hbm,
    proj_hbm,
    proj_bias_hbm,
    text_hbm,
    gain_hbm,
    gate_hbm,
    up_hbm,
    down_hbm,
    out_ref,
    enc_ref,
    frames_ref,
    offset_ref,
    ln_gain_ref,
    ln_bias_ref,
    proj_ref,
    proj_bias_ref,
    text_ref,
    gain_ref,
    gate_w,
    up_w,
    down_w,
    both_w,
    down_p,
    gain_p,
    small,
    audio,
    embedded,
    full,
    products,
    squares,
    parts,
    from_core,
    by_core,
    from_y,
    by_y,
    from_z,
    passed,
    load_sem,
    small_s,
    small_r,
    audio_y_s,
    audio_y_r,
    audio_c_s,
    audio_c_r,
    gz_s,
    gz_r,
    gy_s,
    gy_r,
    gc_s,
    gc_r,
    rc_s,
    rc_r,
    ry_s,
    ry_r,
    rz_s,
    rz_r,
    pass_s,
    pass_r,
):
    f32, bf16 = jnp.float32, jnp.bfloat16
    section = lax.axis_index("section")
    place = lax.axis_index("fsdp")
    core = place % 2
    z = (place // 2) % nz
    y = place // (2 * nz)
    pair = z // 2
    partner = 2 * pair + 1 - z % 2
    pairs = nz // 2
    chunks, rows = full.shape[0], full.shape[4]
    total = chunks * rows
    each = chunks // sections
    last = section // (sections - 1)
    enc_width = enc_ref.shape[-1]
    tiles = enc_width // 128
    hidden_units = gate_w.shape[1]
    half = both_w.shape[-1] // 2
    depth = nz * 128

    def at(y_, z_, core_):
        return (y_ * nz + z_) * 2 + core_

    sibling = at(y, z, 1 - core)

    loads = [
        pltpu.make_async_copy(src, dst, load_sem.at[i])
        for i, (src, dst) in enumerate(
            (
                (enc_hbm, enc_ref),
                (ln_gain_hbm, ln_gain_ref),
                (ln_bias_hbm, ln_bias_ref),
                (frames_hbm, frames_ref),
                (offset_hbm, offset_ref),
                (gain_hbm, gain_ref),
                (down_hbm, down_w),
                (gate_hbm, gate_w),
                (up_hbm, up_w),
                (proj_hbm, proj_ref),
                (proj_bias_hbm, proj_bias_ref),
                (text_hbm, text_ref),
            )
        )
    ]
    for load in loads:
        load.start()

    barrier = pltpu.get_barrier_semaphore()
    greeted = 0
    for ds in range(sections):
        for dz in range(nz):
            if ds or dz:
                pl.semaphore_signal(
                    barrier,
                    inc=1,
                    device_id=((section + ds) % sections, at(y, (z + dz) % nz, core)),
                    device_id_type=MESH,
                )
                greeted += 1
    for dy in range(1, ny):
        pl.semaphore_signal(
            barrier, inc=1, device_id=(section, at((y + dy) % ny, z, core)), device_id_type=MESH
        )
        greeted += 1
    pl.semaphore_signal(barrier, inc=1, device_id=(section, sibling), device_id_type=MESH)
    greeted += 1

    small[z] = jnp.zeros(small.shape[1:], f32)
    for load in loads[:3]:
        load.wait()
    frames = enc_ref[0].astype(f32)
    for j in range(2):
        pooled = 0.5 * (frames[2 * j : 2 * j + 1] + frames[2 * j + 1 : 2 * j + 2])
        centred = pooled - jnp.mean(pooled, axis=-1, keepdims=True)
        spread = jnp.mean(centred * centred, axis=-1, keepdims=True)
        normed = centred * lax.rsqrt(spread + 1e-05)
        for t in range(tiles):
            row = normed[:, t * 128 : (t + 1) * 128] * ln_gain_ref[t : t + 1] + ln_bias_ref[t : t + 1]
            small[z, j * tiles + t : j * tiles + t + 1, :] = row.astype(bf16).astype(f32)
    pl.semaphore_wait(barrier, greeted)

    far_z = near_first(nz)[:0:-1]
    far_y = near_first(ny)[:0:-1]
    sends = []
    arrivals = []
    for d in far_z:
        other = (z + d) % nz
        copy = remote(small.at[z], small.at[z], small_s.at[d], small_r.at[z], section, at(y, other, core))
        copy.start()
        sends.append(copy)
        arrivals.append(
            remote(small.at[other], small.at[other], small_s.at[d], small_r.at[other], section, at(y, other, core))
        )

    for load in loads[3:8]:
        load.wait()
    clips = ny * nz * 2
    row_of = lax.broadcasted_iota(jnp.int32, (clips, 2 * clips), 1)
    clip_of = lax.broadcasted_iota(jnp.int32, (clips, 2 * clips), 0)
    holds = ((row_of // (2 * nz) % ny) * nz + row_of % nz) * 2 + row_of // (2 * nz * ny)
    which = row_of // nz % 2
    spots = jnp.zeros((8, 2 * clips), f32)
    for j in range(2):
        spot = offset_ref[...] + j
        tokens = total // 2
        target = jnp.where(2 * j < frames_ref[...], spot % tokens * 2 + spot // tokens, total)
        order = jnp.where((holds == clip_of) & (which == j), 1.0, 0.0).astype(bf16)
        spread_target = jnp.broadcast_to(target.astype(f32), (8, clips)).astype(bf16)
        spots = spots + jnp.dot(spread_target, order, preferred_element_type=f32)
    slot = lax.broadcasted_iota(jnp.int32, (total, 2 * clips), 0).astype(f32)
    chosen = jnp.where(slot == spots[0:1], 1.0, 0.0)
    taken = jnp.sum(chosen, axis=-1, keepdims=True)
    chosen = chosen.astype(bf16)

    def lanes_of(c, y_, z_):
        return pl.ds(pl.multiple_of(at(y_, z_, c) * 128, 128), 128)

    def arrange_gate(i, carry):
        c, y_ = i // ny, i % ny
        for z_ in range(nz):
            lanes = lanes_of(c, y_, z_)
            here = pl.ds(z_ * 128, 128)
            gain_p[c, y_, :, here] = gain_ref[:, lanes]
            down_p[c, y_, :, here] = down_w[0, :, lanes]
            both_w[c, y_, here, half - 128 : half] = jnp.zeros((128, 128), bf16)
            both_w[c, y_, here, :hidden_units] = gate_w[0, :, lanes].T
        return carry

    def arrange_up(i, carry):
        c, y_ = i // ny, i % ny
        for z_ in range(nz):
            here = pl.ds(z_ * 128, 128)
            both_w[c, y_, here, 2 * half - 128 :] = jnp.zeros((128, 128), bf16)
            both_w[c, y_, here, half : half + hidden_units] = up_w[0, :, lanes_of(c, y_, z_)].T
        return carry

    lax.fori_loop(0, 2 * ny, arrange_gate, 0)

    for copy in arrivals:
        copy.wait_recv()
    for t in range(tiles):
        two = jnp.concatenate([small[:, t, :], small[:, tiles + t, :]], axis=0)
        audio[core, y, :, t * 128 : (t + 1) * 128] = two.astype(bf16)
    arrivals = []
    for d in far_y:
        other = (y + d) % ny
        copy = remote(
            audio.at[core, y], audio.at[core, y], audio_y_s.at[d], audio_y_r.at[y], section, at(other, z, core)
        )
        copy.start()
        sends.append(copy)
        arrivals.append(
            remote(
                audio.at[core, other],
                audio.at[core, other],
                audio_y_s.at[d],
                audio_y_r.at[other],
                section,
                at(other, z, core),
            )
        )
    for load in loads[8:]:
        load.wait()
    lax.fori_loop(0, 2 * ny, arrange_up, 0)
    for copy in arrivals:
        copy.wait_recv()
    copy = remote(audio.at[core], audio.at[core], audio_c_s.at[0], audio_c_r.at[0], section, sibling)
    copy.start()
    sends.append(copy)
    remote(audio.at[1 - core], audio.at[1 - core], audio_c_s.at[0], audio_c_r.at[0], section, sibling).wait_recv()
    gathered = audio[...].reshape(2 * clips, enc_width)
    projected = jnp.dot(gathered, proj_ref[...], preferred_element_type=f32) + proj_bias_ref[...]
    placed = jnp.dot(chosen, projected.astype(bf16), preferred_element_type=f32)
    embedded[...] = jnp.where(taken > 0.0, placed, text_ref[...].astype(f32)).astype(bf16)

    def total_of(k):
        value = passed[k].astype(f32)
        for other in range(nz):
            value = value + from_z[k, other].astype(f32)
        return value.astype(bf16)

    def wait_stream(k):
        for other in range(nz):
            remote(
                from_z.at[k, other], from_z.at[k, other], rz_s.at[0, 0], rz_r.at[k, other], section, sibling
            ).wait_recv()
        remote(passed.at[k], passed.at[k], pass_s.at[0], pass_r.at[k], section, sibling).wait_recv()

    def onward(k):
        to = (section + 1) * (1 - last) + (k // each) * last
        slot_of = k + last * (chunks + k % each - k)
        return to, slot_of

    def begin(k, _):
        own = full.at[k, core, y, z]

        @pl.when(section == 0)
        def _():
            own[...] = embedded[k * rows : (k + 1) * rows, :]

        @pl.when(section > 0)
        def _():
            wait_stream(k)
            own[...] = total_of(k)

        for d in far_z:
            remote(own, own, gz_s.at[k, d], gz_r.at[k, z], section, at(y, (z + d) % nz, core)).start()
        to, slot_of = onward(k)
        if k // each == sections - 1:

            @pl.when(section == sections - 1)
            def _():
                pltpu.make_async_copy(own, passed.at[slot_of], pass_r.at[slot_of]).start()

            @pl.when(section < sections - 1)
            def _():
                remote(own, passed.at[slot_of], pass_s.at[k], pass_r.at[slot_of], to, place).start()

        else:
            remote(own, passed.at[slot_of], pass_s.at[k], pass_r.at[slot_of], to, place).start()

    def gather_y(k, dp):
        p = (pair + dp) % pairs
        for other in (partner,) if dp == 0 else (2 * p, 2 * p + 1):
            block = full.at[k, core, y, other]
            remote(block, block, gz_s.at[k, 0], gz_r.at[k, other], section, sibling).wait_recv()
        block = full.at[k, core, y, pl.ds(2 * p, 2)]
        for d in far_y:
            remote(block, block, gy_s.at[k, d, p], gy_r.at[k, y, p], section, at((y + d) % ny, z, core)).start()

    def multiply(k, c, y_, first):
        squared = None
        scaled = []
        for z_ in range(nz):
            value = full[k, c, y_, z_].astype(f32)
            squared = value * value if squared is None else squared + value * value
            scaled.append((value * gain_p[c, y_, :, z_ * 128 : (z_ + 1) * 128]).astype(bf16))
        product = jnp.dot(jnp.concatenate(scaled, axis=1), both_w[c, y_], preferred_element_type=f32)
        if first:
            squares[k] = squared
            products[k] = product
        else:
            squares[k] += squared
            products[k] += product

    def to_core(k, d):
        other = (y + d) % ny
        if d:
            for p in range(pairs):
                block = full.at[k, core, other, pl.ds(2 * p, 2)]
                remote(block, block, gy_s.at[k, 0, 0], gy_r.at[k, other, p], section, sibling).wait_recv()
        block = full.at[k, core, other]
        remote(block, block, gc_s.at[k, other], gc_r.at[k, other], section, sibling).start()
        multiply(k, core, other, d == 0)

    def of_core(k, d):
        other = (y + d) % ny
        block = full.at[k, 1 - core, other]
        remote(block, block, gc_s.at[k, other], gc_r.at[k, other], section, sibling).wait_recv()
        multiply(k, 1 - core, other, False)

    def down(k, _):
        width = 2 * ny * depth
        scale = lax.rsqrt(jnp.sum(squares[k], axis=-1, keepdims=True) / width + 1e-06)
        gate = products[k, :, :hidden_units] * scale
        up = products[k, :, half : half + hidden_units] * scale
        hidden = (gate / (1.0 + jnp.exp(-gate)) * up).astype(bf16)
        for c in (1 - core, core):
            for d in far_y + [0]:
                other = (y + d) % ny
                value = jnp.dot(hidden, down_p[c, other], preferred_element_type=f32).astype(bf16)
                for z_ in range(nz):
                    parts[k, c, other, z_] = value[:, z_ * 128 : (z_ + 1) * 128]
                if c is not core:
                    remote(
                        parts.at[k, c, other],
                        from_core.at[k, other],
                        rc_s.at[k, other],
                        rc_r.at[k, other],
                        section,
                        sibling,
                    ).start()

    far_pairs = near_first(pairs)[::-1]

    def add_core(k, _):
        for d in far_y + [0]:
            other = (y + d) % ny
            remote(
                parts.at[k, 1 - core, other],
                from_core.at[k, other],
                rc_s.at[k, other],
                rc_r.at[k, other],
                section,
                sibling,
            ).wait_recv()
            by_core[k, other] = (parts[k, core, other].astype(f32) + from_core[k, other].astype(f32)).astype(bf16)
            if d:
                for dp in far_pairs:
                    p = (pair + dp) % pairs
                    remote(
                        by_core.at[k, other, pl.ds(2 * p, 2)],
                        from_y.at[k, d, pl.ds(2 * p, 2)],
                        ry_s.at[k, d, p],
                        ry_r.at[k, d, p],
                        section,
                        at(other, z, core),
                    ).start()

    def sum_y(k, dp):
        p = (pair + dp) % pairs
        for d in range(1, ny):
            block = from_y.at[k, d, pl.ds(2 * p, 2)]
            remote(block, block, ry_s.at[k, d, p], ry_r.at[k, d, p], section, sibling).wait_recv()
        to, slot_of = onward(k)
        for other in (partner, z) if dp == 0 else (2 * p, 2 * p + 1):
            value = by_core[k, y, other].astype(f32)
            for d in range(1, ny):
                value = value + from_y[k, d, other].astype(f32)
            by_y[k, other] = value.astype(bf16)
            copy = remote(
                by_y.at[k, other], from_z.at[slot_of, z], rz_s.at[k, other], rz_r.at[slot_of, z], to, at(y, other, core)
            )
            if other is z and k // each == sections - 1:

                @pl.when(section == sections - 1)
                def _():
                    pltpu.make_async_copy(by_y.at[k, z], from_z.at[slot_of, z], rz_r.at[slot_of, z]).start()

                @pl.when(section < sections - 1)
                def _():
                    copy.start()

            else:
                copy.start()

    steps = [(BEGIN, begin, 0), (OWN, to_core, 0), (FROM_CORE, of_core, 0), (DOWN, down, 0), (ADD_CORE, add_core, 0)]
    for i, dp in enumerate(near_first(pairs)):
        steps.append((PAIR + PAIR_STEP * i, gather_y, dp))
    for i, d in enumerate(near_first(ny)[1:]):
        steps.append((FROM_Y + FROM_Y_STEP * i, to_core, d))
        steps.append((FROM_CORE + FROM_CORE_STEP * (i + 1), of_core, d))
    for i, dp in enumerate(far_pairs):
        steps.append((SUM_Y + SUM_Y_STEP * i, sum_y, dp))
    plan = sorted(
        ((start + INTERVAL * k, k, step, which_one) for start, step, which_one in steps for k in range(chunks)),
        key=lambda entry: entry[:2],
    )
    for _, k, step, which_one in plan:
        step(k, which_one)

    for i in range(each):
        wait_stream(chunks + i)
        out_ref[i * rows : (i + 1) * rows, :] = total_of(chunks + i)

    for copy in sends:
        copy.wait_send()
    for k in range(chunks):
        stays = k // each == sections - 1
        own = full.at[k, core, y, z]
        for d in far_z:
            remote(own, own, gz_s.at[k, d], gz_r.at[k, z], section, sibling).wait_send()
        for p in range(pairs):
            for d in far_y:
                block = full.at[k, core, y, pl.ds(2 * p, 2)]
                remote(block, block, gy_s.at[k, d, p], gy_r.at[k, y, p], section, sibling).wait_send()
                block = by_core.at[k, (y + d) % ny, pl.ds(2 * p, 2)]
                remote(block, block, ry_s.at[k, d, p], ry_r.at[k, d, p], section, sibling).wait_send()
        for y_ in range(ny):
            block = full.at[k, core, y_]
            remote(block, block, gc_s.at[k, y_], gc_r.at[k, y_], section, sibling).wait_send()
            block = parts.at[k, 1 - core, y_]
            remote(block, block, rc_s.at[k, y_], rc_r.at[k, y_], section, sibling).wait_send()
        for d in range(nz):
            other = (z + d) % nz
            block = by_y.at[k, other]
            copy = remote(block, block, rz_s.at[k, other], rz_r.at[k, z], section, sibling)
            if d == 0 and stays:
                pl.when(section < sections - 1)(copy.wait_send)
            else:
                copy.wait_send()
        copy = remote(own, passed.at[k], pass_s.at[k], pass_r.at[k], section, sibling)
        if stays:
            pl.when(section < sections - 1)(copy.wait_send)
        else:
            copy.wait_send()


def on_device(
    sections,
    ny,
    nz,
    enc_states,
    clip_frames,
    clip_offset,
    ln_gain,
    ln_bias,
    w_proj,
    proj_bias,
    text_embed,
    norm_gain,
    w_gate,
    w_up,
    w_down,
):
    tokens, micro, feat = text_embed.shape
    total = tokens * micro
    hidden_units, width = w_gate.shape[1:]
    chunks = CHUNKS
    rows = total // chunks
    each = chunks // sections
    enc_width = enc_states.shape[-1]
    small_rows = -(-2 * (enc_width // 128) // 8) * 8
    half = -(-hidden_units // 128) * 128
    bf16, f32 = jnp.bfloat16, jnp.float32
    hbm = pl.BlockSpec(memory_space=pl.ANY)
    dma = pltpu.SemaphoreType.DMA
    args = (
        enc_states,
        clip_frames.reshape(1, -1),
        clip_offset.reshape(1, -1),
        ln_gain.reshape(-1, 128),
        ln_bias.reshape(-1, 128),
        w_proj,
        proj_bias.reshape(1, -1),
        text_embed.reshape(total, feat),
        norm_gain,
        w_gate,
        w_up,
        w_down,
    )
    out = pl.pallas_call(
        functools.partial(kernel, sections, ny, nz),
        out_shape=jax.ShapeDtypeStruct((total // sections, feat), bf16),
        in_specs=[hbm] * len(args),
        out_specs=pl.BlockSpec(memory_space=pltpu.VMEM),
        scratch_shapes=[pltpu.VMEM(arg.shape, arg.dtype) for arg in args]
        + [
            pltpu.VMEM((2, ny, nz * feat, 2 * half), bf16),
            pltpu.VMEM((2, ny, hidden_units, nz * feat), bf16),
            pltpu.VMEM((2, ny, 1, nz * feat), f32),
            pltpu.VMEM((nz, small_rows, 128), f32),
            pltpu.VMEM((2, ny, 2 * nz, enc_width), bf16),
            pltpu.VMEM((total, feat), bf16),
            pltpu.VMEM((chunks, 2, ny, nz, rows, feat), bf16),
            pltpu.VMEM((chunks, rows, 2 * half), f32),
            pltpu.VMEM((chunks, rows, feat), f32),
            pltpu.VMEM((chunks, 2, ny, nz, rows, feat), bf16),
            pltpu.VMEM((chunks, ny, nz, rows, feat), bf16),
            pltpu.VMEM((chunks, ny, nz, rows, feat), bf16),
            pltpu.VMEM((chunks, ny, nz, rows, feat), bf16),
            pltpu.VMEM((chunks, nz, rows, feat), bf16),
            pltpu.VMEM((chunks + each, nz, rows, feat), bf16),
            pltpu.VMEM((chunks + each, rows, feat), bf16),
            dma((len(args),)),
            dma((nz,)),
            dma((nz,)),
            dma((ny,)),
            dma((ny,)),
            dma((1,)),
            dma((1,)),
            dma((chunks, nz)),
            dma((chunks, nz)),
            dma((chunks, ny, nz // 2)),
            dma((chunks, ny, nz // 2)),
            dma((chunks, ny)),
            dma((chunks, ny)),
            dma((chunks, ny)),
            dma((chunks, ny)),
            dma((chunks, ny, nz // 2)),
            dma((chunks, ny, nz // 2)),
            dma((chunks, nz)),
            dma((chunks + each, nz)),
            dma((chunks,)),
            dma((chunks + each,)),
        ],
        compiler_params=pltpu.CompilerParams(
            collective_id=0, has_side_effects=True, vmem_limit_bytes=62 * 2**20
        ),
        cost_estimate=pl.CostEstimate(
            flops=6 * total * hidden_units * width, bytes_accessed=6 * hidden_units * width, transcendentals=0
        ),
    )(*args)
    return out.reshape(tokens // sections, micro, feat)


def solution(mesh):
    sections, spread = mesh.shape["section"], mesh.shape["fsdp"]
    ny = 4 if spread == 64 else 2
    nz = spread // (2 * ny)
    placed = (
        P("fsdp", None, None),
        P(),
        P(),
        P(),
        P(),
        P(None, "fsdp"),
        P("fsdp"),
        P(None, None, "fsdp"),
        P("section", None),
        P("section", "fsdp", None),
        P("section", "fsdp", None),
        P("section", "fsdp", None),
    )
    return jax.shard_map(
        functools.partial(on_device, sections, ny, nz),
        mesh=mesh,
        in_specs=placed,
        out_specs=P("section", None, "fsdp"),
        check_vma=False,
    )
```

```python
import functools

import jax
import jax.numpy as jnp
from jax import lax
from jax.experimental import pallas as pl
from jax.experimental.pallas import tpu as pltpu
from jax.sharding import PartitionSpec as P

MESH = pl.DeviceIdType.MESH
CHUNKS = 4
ORDER = (
    0, 0, 0, 0, 0, 1, 0, 1, 0, 0, 1, 1, 1, 0, 0, 0, 0, 0, 0, 2, 1, 1, 1, 0, 1, 1, 1, 1, 2, 1, 2, 2, 2, 1, 3, 1, 0, 0,
    0, 0, 2, 2, 2, 3, 2, 2, 3, 3, 3, 2, 2, 2, 1, 1, 1, 1, 2, 3, 2, 3, 3, 3, 3, 3, 3, 3, 3, 3, 2, 2, 2, 2, 3, 3, 3, 3,
)


def near_first(count):
    return sorted(range(count), key=lambda d: (min(d, count - d), d))


def remote(src, dst, send, recv, section, place):
    return pltpu.make_async_remote_copy(
        src_ref=src,
        dst_ref=dst,
        send_sem=send,
        recv_sem=recv,
        device_id=(section, place),
        device_id_type=MESH,
    )


def kernel(
    sections,
    ny,
    nz,
    enc_hbm,
    frames_hbm,
    offset_hbm,
    ln_gain_hbm,
    ln_bias_hbm,
    proj_hbm,
    proj_bias_hbm,
    text_hbm,
    gain_hbm,
    gate_hbm,
    up_hbm,
    down_hbm,
    out_ref,
    enc_ref,
    frames_ref,
    offset_ref,
    ln_gain_ref,
    ln_bias_ref,
    proj_ref,
    proj_bias_ref,
    text_ref,
    gain_ref,
    gate_w,
    up_w,
    down_w,
    both_w,
    down_p,
    gain_p,
    small,
    audio,
    embedded,
    full,
    products,
    squares,
    parts,
    from_core,
    by_core,
    from_y,
    by_y,
    from_z,
    passed,
    load_sem,
    small_s,
    small_r,
    audio_y_s,
    audio_y_r,
    audio_c_s,
    audio_c_r,
    gz_s,
    gz_r,
    gy_s,
    gy_r,
    gc_s,
    gc_r,
    rc_s,
    rc_r,
    ry_s,
    ry_r,
    rz_s,
    rz_r,
    pass_s,
    pass_r,
):
    f32, bf16 = jnp.float32, jnp.bfloat16
    section = lax.axis_index("section")
    place = lax.axis_index("fsdp")
    core = place % 2
    z = (place // 2) % nz
    y = place // (2 * nz)
    pair = z // 2
    partner = 2 * pair + 1 - z % 2
    pairs = nz // 2
    chunks, rows = full.shape[0], full.shape[4]
    total = chunks * rows
    each = chunks // sections
    last = section // (sections - 1)
    enc_width = enc_ref.shape[-1]
    tiles = enc_width // 128
    hidden_units = gate_w.shape[1]
    half = both_w.shape[-1] // 2
    depth = nz * 128

    def at(y_, z_, core_):
        return (y_ * nz + z_) * 2 + core_

    sibling = at(y, z, 1 - core)

    loads = [
        pltpu.make_async_copy(src, dst, load_sem.at[i])
        for i, (src, dst) in enumerate(
            (
                (enc_hbm, enc_ref),
                (ln_gain_hbm, ln_gain_ref),
                (ln_bias_hbm, ln_bias_ref),
                (frames_hbm, frames_ref),
                (offset_hbm, offset_ref),
                (gain_hbm, gain_ref),
                (down_hbm, down_w),
                (gate_hbm, gate_w),
                (up_hbm, up_w),
                (proj_hbm, proj_ref),
                (proj_bias_hbm, proj_bias_ref),
                (text_hbm, text_ref),
            )
        )
    ]
    for load in loads:
        load.start()

    barrier = pltpu.get_barrier_semaphore()
    greeted = 0
    for ds in range(sections):
        for dz in range(nz):
            if ds or dz:
                pl.semaphore_signal(
                    barrier,
                    inc=1,
                    device_id=((section + ds) % sections, at(y, (z + dz) % nz, core)),
                    device_id_type=MESH,
                )
                greeted += 1
    for dy in range(1, ny):
        pl.semaphore_signal(
            barrier, inc=1, device_id=(section, at((y + dy) % ny, z, core)), device_id_type=MESH
        )
        greeted += 1
    pl.semaphore_signal(barrier, inc=1, device_id=(section, sibling), device_id_type=MESH)
    greeted += 1

    small[z] = jnp.zeros(small.shape[1:], f32)
    for load in loads[:3]:
        load.wait()
    frames = enc_ref[0].astype(f32)
    for j in range(2):
        pooled = 0.5 * (frames[2 * j : 2 * j + 1] + frames[2 * j + 1 : 2 * j + 2])
        centred = pooled - jnp.mean(pooled, axis=-1, keepdims=True)
        spread = jnp.mean(centred * centred, axis=-1, keepdims=True)
        normed = centred * lax.rsqrt(spread + 1e-05)
        for t in range(tiles):
            row = normed[:, t * 128 : (t + 1) * 128] * ln_gain_ref[t : t + 1] + ln_bias_ref[t : t + 1]
            small[z, j * tiles + t : j * tiles + t + 1, :] = row.astype(bf16).astype(f32)
    pl.semaphore_wait(barrier, greeted)

    far_z = near_first(nz)[:0:-1]
    far_y = near_first(ny)[:0:-1]
    for d in far_z:
        other = (z + d) % nz
        copy = remote(small.at[z], small.at[z], small_s.at[0], small_r.at[0], section, at(y, other, core))
        copy.start()

    for load in loads[3:8]:
        load.wait()
    clips = ny * nz * 2
    row_of = lax.broadcasted_iota(jnp.int32, (clips, 2 * clips), 1)
    clip_of = lax.broadcasted_iota(jnp.int32, (clips, 2 * clips), 0)
    holds = ((row_of // (2 * nz) % ny) * nz + row_of % nz) * 2 + row_of // (2 * nz * ny)
    which = row_of // nz % 2
    spots = jnp.zeros((8, 2 * clips), f32)
    for j in range(2):
        spot = offset_ref[...] + j
        tokens = total // 2
        target = jnp.where(2 * j < frames_ref[...], spot % tokens * 2 + spot // tokens, total)
        order = jnp.where((holds == clip_of) & (which == j), 1.0, 0.0).astype(bf16)
        spread_target = jnp.broadcast_to(target.astype(f32), (8, clips)).astype(bf16)
        spots = spots + jnp.dot(spread_target, order, preferred_element_type=f32)
    slot = lax.broadcasted_iota(jnp.int32, (total, 2 * clips), 0).astype(f32)
    chosen = jnp.where(slot == spots[0:1], 1.0, 0.0)
    taken = jnp.sum(chosen, axis=-1, keepdims=True)
    chosen = chosen.astype(bf16)

    def lanes_of(c, y_, z_):
        return pl.ds(pl.multiple_of(at(y_, z_, c) * 128, 128), 128)

    def arrange_gate(i, carry):
        c, y_ = i // ny, i % ny
        for z_ in range(nz):
            lanes = lanes_of(c, y_, z_)
            here = pl.ds(z_ * 128, 128)
            gain_p[c, y_, :, here] = gain_ref[:, lanes]
            down_p[c, y_, :, here] = down_w[0, :, lanes]
            both_w[c, y_, here, half - 128 : half] = jnp.zeros((128, 128), bf16)
            both_w[c, y_, here, :hidden_units] = gate_w[0, :, lanes].T
        return carry

    def arrange_up(i, carry):
        c, y_ = i // ny, i % ny
        for z_ in range(nz):
            here = pl.ds(z_ * 128, 128)
            both_w[c, y_, here, 2 * half - 128 :] = jnp.zeros((128, 128), bf16)
            both_w[c, y_, here, half : half + hidden_units] = up_w[0, :, lanes_of(c, y_, z_)].T
        return carry

    lax.fori_loop(0, 2 * ny, arrange_gate, 0)

    block = small.at[pl.ds(0, nz - 1)]
    remote(block, block, small_s.at[0], small_r.at[0], section, sibling).wait_recv()
    for t in range(tiles):
        two = jnp.concatenate([small[:, t, :], small[:, tiles + t, :]], axis=0)
        audio[core, y, :, t * 128 : (t + 1) * 128] = two.astype(bf16)
    for d in far_y:
        block = audio.at[core, y]
        remote(block, block, audio_y_s.at[0], audio_y_r.at[0], section, at((y + d) % ny, z, core)).start()
    for load in loads[8:]:
        load.wait()
    lax.fori_loop(0, 2 * ny, arrange_up, 0)
    block = audio.at[core, pl.ds(0, ny - 1)]
    remote(block, block, audio_y_s.at[0], audio_y_r.at[0], section, sibling).wait_recv()
    copy = remote(audio.at[core], audio.at[core], audio_c_s.at[0], audio_c_r.at[0], section, sibling)
    copy.start()
    remote(audio.at[1 - core], audio.at[1 - core], audio_c_s.at[0], audio_c_r.at[0], section, sibling).wait_recv()
    gathered = audio[...].reshape(2 * clips, enc_width)
    projected = jnp.dot(gathered, proj_ref[...], preferred_element_type=f32) + proj_bias_ref[...]
    placed = jnp.dot(chosen, projected.astype(bf16), preferred_element_type=f32)
    embedded[...] = jnp.where(taken > 0.0, placed, text_ref[...].astype(f32)).astype(bf16)

    def total_of(k):
        value = passed[k].astype(f32)
        for other in range(nz):
            value = value + from_z[k, other].astype(f32)
        return value.astype(bf16)

    def wait_stream(k):
        remote(from_z.at[k], from_z.at[k], rz_s.at[0], rz_r.at[k], section, sibling).wait_recv()
        remote(passed.at[k], passed.at[k], pass_s.at[0], pass_r.at[k], section, sibling).wait_recv()

    def onward(k):
        to = (section + 1) * (1 - last) + (k // each) * last
        slot_of = k + last * (chunks + k % each - k)
        return to, slot_of

    def begin(k, _):
        own = full.at[k, core, y, z]

        @pl.when(section == 0)
        def _():
            own[...] = embedded[k * rows : (k + 1) * rows, :]

        @pl.when(section > 0)
        def _():
            wait_stream(k)
            own[...] = total_of(k)

        for d in far_z:
            remote(own, own, gz_s.at[0], gz_r.at[k, pair], section, at(y, (z + d) % nz, core)).start()
        to, slot_of = onward(k)
        if k // each == sections - 1:

            @pl.when(section == sections - 1)
            def _():
                pltpu.make_async_copy(own, passed.at[slot_of], pass_r.at[slot_of]).start()

            @pl.when(section < sections - 1)
            def _():
                remote(own, passed.at[slot_of], pass_s.at[0], pass_r.at[slot_of], to, place).start()

        else:
            remote(own, passed.at[slot_of], pass_s.at[0], pass_r.at[slot_of], to, place).start()

    def gather_y(k, dp):
        p = (pair + dp) % pairs
        block = full.at[k, core, y, partner] if dp == 0 else full.at[k, core, y, pl.ds(2 * p, 2)]
        remote(block, block, gz_s.at[0], gz_r.at[k, p], section, sibling).wait_recv()
        block = full.at[k, core, y, pl.ds(2 * p, 2)]
        for d in far_y:
            remote(block, block, gy_s.at[0], gy_r.at[k, y], section, at((y + d) % ny, z, core)).start()

    def multiply(k, c, y_, first):
        squared = None
        scaled = []
        for z_ in range(nz):
            value = full[k, c, y_, z_].astype(f32)
            squared = value * value if squared is None else squared + value * value
            scaled.append((value * gain_p[c, y_, :, z_ * 128 : (z_ + 1) * 128]).astype(bf16))
        product = jnp.dot(jnp.concatenate(scaled, axis=1), both_w[c, y_], preferred_element_type=f32)
        if first:
            squares[k] = squared
            products[k] = product
        else:
            squares[k] += squared
            products[k] += product

    def to_core(k, d):
        other = (y + d) % ny
        block = full.at[k, core, other]
        if d:
            remote(block, block, gy_s.at[0], gy_r.at[k, other], section, sibling).wait_recv()
        remote(block, block, gc_s.at[0], gc_r.at[k, other], section, sibling).start()
        multiply(k, core, other, d == 0)

    def of_core(k, d):
        other = (y + d) % ny
        block = full.at[k, 1 - core, other]
        remote(block, block, gc_s.at[0], gc_r.at[k, other], section, sibling).wait_recv()
        multiply(k, 1 - core, other, False)

    def down(k, _):
        width = 2 * ny * depth
        scale = lax.rsqrt(jnp.sum(squares[k], axis=-1, keepdims=True) / width + 1e-06)
        gate = products[k, :, :hidden_units] * scale
        up = products[k, :, half : half + hidden_units] * scale
        hidden = (gate / (1.0 + jnp.exp(-gate)) * up).astype(bf16)
        for c in (1 - core, core):
            for d in far_y + [0]:
                other = (y + d) % ny
                value = jnp.dot(hidden, down_p[c, other], preferred_element_type=f32).astype(bf16)
                for z_ in range(nz):
                    parts[k, c, other, z_] = value[:, z_ * 128 : (z_ + 1) * 128]
                if c is not core:
                    remote(
                        parts.at[k, c, other],
                        from_core.at[k, other],
                        rc_s.at[0],
                        rc_r.at[k, other],
                        section,
                        sibling,
                    ).start()

    far_pairs = near_first(pairs)[::-1]

    def add_core(k, _):
        for d in far_y + [0]:
            other = (y + d) % ny
            remote(
                parts.at[k, 1 - core, other],
                from_core.at[k, other],
                rc_s.at[0],
                rc_r.at[k, other],
                section,
                sibling,
            ).wait_recv()
            by_core[k, other] = (parts[k, core, other].astype(f32) + from_core[k, other].astype(f32)).astype(bf16)
            if d:
                for dp in far_pairs:
                    p = (pair + dp) % pairs
                    remote(
                        by_core.at[k, other, pl.ds(2 * p, 2)],
                        from_y.at[k, p, d - 1],
                        ry_s.at[0],
                        ry_r.at[k, p],
                        section,
                        at(other, z, core),
                    ).start()

    def sum_y(k, dp):
        p = (pair + dp) % pairs
        block = from_y.at[k, p]
        remote(block, block, ry_s.at[0], ry_r.at[k, p], section, sibling).wait_recv()
        to, slot_of = onward(k)
        for other in (partner, z) if dp == 0 else (2 * p, 2 * p + 1):
            value = by_core[k, y, other].astype(f32)
            for d in range(1, ny):
                value = value + from_y[k, p, d - 1, other % 2].astype(f32)
            by_y[k, other] = value.astype(bf16)
            copy = remote(
                by_y.at[k, other], from_z.at[slot_of, z], rz_s.at[0], rz_r.at[slot_of], to, at(y, other, core)
            )
            if other is z and k // each == sections - 1:

                @pl.when(section == sections - 1)
                def _():
                    pltpu.make_async_copy(by_y.at[k, z], from_z.at[slot_of, z], rz_r.at[slot_of]).start()

                @pl.when(section < sections - 1)
                def _():
                    copy.start()

            else:
                copy.start()

    steps = [(begin, 0)]
    steps += [(gather_y, dp) for dp in near_first(pairs)]
    steps += [(to_core, d) for d in near_first(ny)]
    steps += [(of_core, d) for d in near_first(ny)]
    steps += [(down, 0), (add_core, 0)]
    steps += [(sum_y, dp) for dp in far_pairs]
    order = ORDER if len(ORDER) == chunks * len(steps) else tuple(range(chunks)) * len(steps)
    taken_steps = [0] * chunks
    for k in order:
        step, which_one = steps[taken_steps[k]]
        taken_steps[k] += 1
        step(k, which_one)

    def sent(block, sem):
        remote(block, block, sem, pass_r.at[0], section, sibling).wait_send()

    sent(small.at[pl.ds(0, nz - 1)], small_s.at[0])
    sent(audio.at[core, pl.ds(0, ny - 1)], audio_y_s.at[0])
    sent(audio.at[core], audio_c_s.at[0])
    sent(full.at[:, core, y, pl.ds(0, nz - 1)], gz_s.at[0])
    sent(full.at[:, core, pl.ds(0, ny - 1)], gy_s.at[0])
    sent(full.at[:, core], gc_s.at[0])
    sent(from_core.at[...], rc_s.at[0])
    sent(by_core.at[:, pl.ds(0, ny - 1)], ry_s.at[0])

    @pl.when(section < sections - 1)
    def _():
        sent(by_y.at[...], rz_s.at[0])
        sent(passed.at[pl.ds(0, chunks)], pass_s.at[0])

    @pl.when(section == sections - 1)
    def _():
        sent(by_y.at[pl.ds(0, chunks - each)], rz_s.at[0])
        sent(by_y.at[pl.ds(0, each), pl.ds(0, nz - 1)], rz_s.at[0])
        sent(passed.at[pl.ds(0, chunks - each)], pass_s.at[0])

    for i in range(each):
        wait_stream(chunks + i)
        out_ref[i * rows : (i + 1) * rows, :] = total_of(chunks + i)


def on_device(
    sections,
    ny,
    nz,
    enc_states,
    clip_frames,
    clip_offset,
    ln_gain,
    ln_bias,
    w_proj,
    proj_bias,
    text_embed,
    norm_gain,
    w_gate,
    w_up,
    w_down,
):
    tokens, micro, feat = text_embed.shape
    total = tokens * micro
    hidden_units, width = w_gate.shape[1:]
    chunks = CHUNKS
    rows = total // chunks
    each = chunks // sections
    enc_width = enc_states.shape[-1]
    small_rows = -(-2 * (enc_width // 128) // 8) * 8
    half = -(-hidden_units // 128) * 128
    bf16, f32 = jnp.bfloat16, jnp.float32
    hbm = pl.BlockSpec(memory_space=pl.ANY)
    dma = pltpu.SemaphoreType.DMA
    args = (
        enc_states,
        clip_frames.reshape(1, -1),
        clip_offset.reshape(1, -1),
        ln_gain.reshape(-1, 128),
        ln_bias.reshape(-1, 128),
        w_proj,
        proj_bias.reshape(1, -1),
        text_embed.reshape(total, feat),
        norm_gain,
        w_gate,
        w_up,
        w_down,
    )
    out = pl.pallas_call(
        functools.partial(kernel, sections, ny, nz),
        out_shape=jax.ShapeDtypeStruct((total // sections, feat), bf16),
        in_specs=[hbm] * len(args),
        out_specs=pl.BlockSpec(memory_space=pltpu.VMEM),
        scratch_shapes=[pltpu.VMEM(arg.shape, arg.dtype) for arg in args]
        + [
            pltpu.VMEM((2, ny, nz * feat, 2 * half), bf16),
            pltpu.VMEM((2, ny, hidden_units, nz * feat), bf16),
            pltpu.VMEM((2, ny, 1, nz * feat), f32),
            pltpu.VMEM((nz, small_rows, 128), f32),
            pltpu.VMEM((2, ny, 2 * nz, enc_width), bf16),
            pltpu.VMEM((total, feat), bf16),
            pltpu.VMEM((chunks, 2, ny, nz, rows, feat), bf16),
            pltpu.VMEM((chunks, rows, 2 * half), f32),
            pltpu.VMEM((chunks, rows, feat), f32),
            pltpu.VMEM((chunks, 2, ny, nz, rows, feat), bf16),
            pltpu.VMEM((chunks, ny, nz, rows, feat), bf16),
            pltpu.VMEM((chunks, ny, nz, rows, feat), bf16),
            pltpu.VMEM((chunks, nz // 2, ny - 1, 2, rows, feat), bf16),
            pltpu.VMEM((chunks, nz, rows, feat), bf16),
            pltpu.VMEM((chunks + each, nz, rows, feat), bf16),
            pltpu.VMEM((chunks + each, rows, feat), bf16),
            dma((len(args),)),
            dma((1,)),
            dma((1,)),
            dma((1,)),
            dma((1,)),
            dma((1,)),
            dma((1,)),
            dma((1,)),
            dma((chunks, nz // 2)),
            dma((1,)),
            dma((chunks, ny)),
            dma((1,)),
            dma((chunks, ny)),
            dma((1,)),
            dma((chunks, ny)),
            dma((1,)),
            dma((chunks, nz // 2)),
            dma((1,)),
            dma((chunks + each,)),
            dma((1,)),
            dma((chunks + each,)),
        ],
        compiler_params=pltpu.CompilerParams(
            collective_id=0, has_side_effects=True, vmem_limit_bytes=62 * 2**20
        ),
        cost_estimate=pl.CostEstimate(
            flops=6 * total * hidden_units * width, bytes_accessed=6 * hidden_units * width, transcendentals=0
        ),
    )(*args)
    return out.reshape(tokens // sections, micro, feat)


def solution(mesh):
    sections, spread = mesh.shape["section"], mesh.shape["fsdp"]
    ny = 4 if spread == 64 else 2
    nz = spread // (2 * ny)
    placed = (
        P("fsdp", None, None),
        P(),
        P(),
        P(),
        P(),
        P(None, "fsdp"),
        P("fsdp"),
        P(None, None, "fsdp"),
        P("section", None),
        P("section", "fsdp", None),
        P("section", "fsdp", None),
        P("section", "fsdp", None),
    )
    return jax.shard_map(
        functools.partial(on_device, sections, ny, nz),
        mesh=mesh,
        in_specs=placed,
        out_specs=P("section", None, "fsdp"),
        check_vma=False,
    )
```

```python
import functools

import jax
import jax.numpy as jnp
from jax import lax
from jax.experimental import pallas as pl
from jax.experimental.pallas import tpu as pltpu
from jax.sharding import PartitionSpec as P

MESH = pl.DeviceIdType.MESH
CHUNKS = 4
ORDER = (
    0, 0, 0, 0, 0, 1, 0, 1, 0, 0, 1, 1, 1, 0, 0, 0, 0, 0, 0, 2, 1, 1, 1, 0, 1, 1, 1, 1, 2, 1, 2, 2, 2, 1, 3, 1, 0, 0,
    0, 0, 2, 2, 2, 3, 2, 2, 3, 3, 3, 2, 2, 2, 1, 1, 1, 1, 2, 3, 2, 3, 3, 3, 3, 3, 3, 3, 3, 3, 2, 2, 2, 2, 3, 3, 3, 3,
)


def near_first(count):
    return sorted(range(count), key=lambda d: (min(d, count - d), d))


def remote(src, dst, send, recv, section, place):
    return pltpu.make_async_remote_copy(
        src_ref=src,
        dst_ref=dst,
        send_sem=send,
        recv_sem=recv,
        device_id=(section, place),
        device_id_type=MESH,
    )


def kernel(
    sections,
    ny,
    nz,
    enc_hbm,
    frames_hbm,
    offset_hbm,
    ln_gain_hbm,
    ln_bias_hbm,
    proj_hbm,
    proj_bias_hbm,
    text_hbm,
    gain_hbm,
    gate_hbm,
    up_hbm,
    down_hbm,
    out_ref,
    enc_ref,
    frames_ref,
    offset_ref,
    ln_gain_ref,
    ln_bias_ref,
    proj_ref,
    proj_bias_ref,
    text_ref,
    gain_ref,
    gate_w,
    up_w,
    down_w,
    both_w,
    down_p,
    gain_p,
    small,
    audio,
    embedded,
    full,
    products,
    squares,
    parts,
    from_core,
    by_core,
    from_y,
    by_y,
    from_z,
    passed,
    load_sem,
    small_s,
    small_r,
    audio_y_s,
    audio_y_r,
    audio_c_s,
    audio_c_r,
    gz_s,
    gz_r,
    gy_s,
    gy_r,
    gc_s,
    gc_r,
    rc_s,
    rc_r,
    ry_s,
    ry_r,
    rz_s,
    rz_r,
    pass_s,
    pass_r,
):
    f32, bf16 = jnp.float32, jnp.bfloat16
    section = lax.axis_index("section")
    place = lax.axis_index("fsdp")
    core = place % 2
    z = (place // 2) % nz
    y = place // (2 * nz)
    pair = z // 2
    partner = 2 * pair + 1 - z % 2
    pairs = nz // 2
    chunks, rows = full.shape[0], full.shape[4]
    total = chunks * rows
    each = chunks // sections
    last = section // (sections - 1)
    enc_width = enc_ref.shape[-1]
    tiles = enc_width // 128
    hidden_units = gate_w.shape[1]
    half = both_w.shape[-1] // 2
    depth = nz * 128

    def at(y_, z_, core_):
        return (y_ * nz + z_) * 2 + core_

    sibling = at(y, z, 1 - core)

    loads = [
        pltpu.make_async_copy(src, dst, load_sem.at[i])
        for i, (src, dst) in enumerate(
            (
                (enc_hbm, enc_ref),
                (ln_gain_hbm, ln_gain_ref),
                (ln_bias_hbm, ln_bias_ref),
                (frames_hbm, frames_ref),
                (offset_hbm, offset_ref),
                (gain_hbm, gain_ref),
                (down_hbm, down_w),
                (gate_hbm, gate_w),
                (up_hbm, up_w),
                (proj_hbm, proj_ref),
                (proj_bias_hbm, proj_bias_ref),
                (text_hbm, text_ref),
            )
        )
    ]
    for load in loads[:3]:
        load.start()

    barrier = pltpu.get_barrier_semaphore()

    def greet(section_, places):
        for place_ in places:
            pl.semaphore_signal(barrier, inc=1, device_id=(section_, place_), device_id_type=MESH)
        return len(places)

    beside = [at(y, (z + d) % nz, core) for d in range(1, nz)]
    onwards = greet((section + sections - 1) % sections, [place] + beside)
    greeted = greet(section, beside + [at((y + d) % ny, z, core) for d in range(1, ny)] + [sibling])

    @pl.when((section > 0) & (section < sections - 1))
    def _():
        greet(sections - 1, [place] + beside)

    for load in loads[3:]:
        load.start()

    small[z] = jnp.zeros(small.shape[1:], f32)
    for load in loads[:3]:
        load.wait()
    frames = enc_ref[0].astype(f32)
    for j in range(2):
        pooled = 0.5 * (frames[2 * j : 2 * j + 1] + frames[2 * j + 1 : 2 * j + 2])
        centred = pooled - jnp.mean(pooled, axis=-1, keepdims=True)
        spread = jnp.mean(centred * centred, axis=-1, keepdims=True)
        normed = centred * lax.rsqrt(spread + 1e-05)
        for t in range(tiles):
            row = normed[:, t * 128 : (t + 1) * 128] * ln_gain_ref[t : t + 1] + ln_bias_ref[t : t + 1]
            small[z, j * tiles + t : j * tiles + t + 1, :] = row.astype(bf16).astype(f32)
    pl.semaphore_wait(barrier, greeted + onwards * (1 + (sections - 2) * last))

    far_z = near_first(nz)[:0:-1]
    far_y = near_first(ny)[:0:-1]
    for d in far_z:
        other = (z + d) % nz
        copy = remote(small.at[z], small.at[z], small_s.at[0], small_r.at[0], section, at(y, other, core))
        copy.start()

    for load in loads[3:8]:
        load.wait()
    clips = ny * nz * 2
    row_of = lax.broadcasted_iota(jnp.int32, (clips, 2 * clips), 1)
    clip_of = lax.broadcasted_iota(jnp.int32, (clips, 2 * clips), 0)
    holds = ((row_of // (2 * nz) % ny) * nz + row_of % nz) * 2 + row_of // (2 * nz * ny)
    which = row_of // nz % 2
    spots = jnp.zeros((8, 2 * clips), f32)
    for j in range(2):
        spot = offset_ref[...] + j
        tokens = total // 2
        target = jnp.where(2 * j < frames_ref[...], spot % tokens * 2 + spot // tokens, total)
        order = jnp.where((holds == clip_of) & (which == j), 1.0, 0.0).astype(bf16)
        spread_target = jnp.broadcast_to(target.astype(f32), (8, clips)).astype(bf16)
        spots = spots + jnp.dot(spread_target, order, preferred_element_type=f32)
    slot = lax.broadcasted_iota(jnp.int32, (total, 2 * clips), 0).astype(f32)
    chosen = jnp.where(slot == spots[0:1], 1.0, 0.0)
    taken = jnp.sum(chosen, axis=-1, keepdims=True)
    chosen = chosen.astype(bf16)

    def lanes_of(c, y_, z_):
        return pl.ds(pl.multiple_of(at(y_, z_, c) * 128, 128), 128)

    def arrange_gate(i, carry):
        c, y_ = i // ny, i % ny
        for z_ in range(nz):
            lanes = lanes_of(c, y_, z_)
            here = pl.ds(z_ * 128, 128)
            gain_p[c, y_, :, here] = gain_ref[:, lanes]
            down_p[c, y_, :, here] = down_w[0, :, lanes]
            both_w[c, y_, here, half - 128 : half] = jnp.zeros((128, 128), bf16)
            both_w[c, y_, here, :hidden_units] = gate_w[0, :, lanes].T
        return carry

    def arrange_up(i, carry):
        c, y_ = i // ny, i % ny
        for z_ in range(nz):
            here = pl.ds(z_ * 128, 128)
            both_w[c, y_, here, 2 * half - 128 :] = jnp.zeros((128, 128), bf16)
            both_w[c, y_, here, half : half + hidden_units] = up_w[0, :, lanes_of(c, y_, z_)].T
        return carry

    lax.fori_loop(0, 2 * ny, arrange_gate, 0)

    block = small.at[pl.ds(0, nz - 1)]
    remote(block, block, small_s.at[0], small_r.at[0], section, sibling).wait_recv()
    for t in range(tiles):
        two = jnp.concatenate([small[:, t, :], small[:, tiles + t, :]], axis=0)
        audio[core, y, :, t * 128 : (t + 1) * 128] = two.astype(bf16)
    for d in far_y:
        block = audio.at[core, y]
        remote(block, block, audio_y_s.at[0], audio_y_r.at[y], section, at((y + d) % ny, z, core)).start()
    remote(block, block, audio_c_s.at[0], audio_c_r.at[0], section, sibling).start()
    for load in loads[8:]:
        load.wait()
    lax.fori_loop(0, 2 * ny, arrange_up, 0)
    for d in far_y[::-1]:
        other = (y + d) % ny
        block = audio.at[core, other]
        remote(block, block, audio_y_s.at[0], audio_y_r.at[other], section, sibling).wait_recv()
        remote(block, block, audio_c_s.at[0], audio_c_r.at[0], section, sibling).start()
    block = audio.at[1 - core]
    remote(block, block, audio_c_s.at[0], audio_c_r.at[0], section, sibling).wait_recv()
    gathered = audio[...].reshape(2 * clips, enc_width)
    projected = jnp.dot(gathered, proj_ref[...], preferred_element_type=f32) + proj_bias_ref[...]
    placed = jnp.dot(chosen, projected.astype(bf16), preferred_element_type=f32)
    embedded[...] = jnp.where(taken > 0.0, placed, text_ref[...].astype(f32)).astype(bf16)

    def total_of(k):
        value = passed[k].astype(f32)
        for other in range(nz):
            value = value + from_z[k, other].astype(f32)
        return value.astype(bf16)

    def wait_stream(k):
        remote(from_z.at[k], from_z.at[k], rz_s.at[0], rz_r.at[k], section, sibling).wait_recv()
        remote(passed.at[k], passed.at[k], pass_s.at[0], pass_r.at[k], section, sibling).wait_recv()

    def onward(k):
        to = (section + 1) * (1 - last) + (k // each) * last
        slot_of = k + last * (chunks + k % each - k)
        return to, slot_of

    def begin(k, _):
        own = full.at[k, core, y, z]

        @pl.when(section == 0)
        def _():
            own[...] = embedded[k * rows : (k + 1) * rows, :]

        @pl.when(section > 0)
        def _():
            wait_stream(k)
            own[...] = total_of(k)

        for d in far_z:
            remote(own, own, gz_s.at[0], gz_r.at[k, pair], section, at(y, (z + d) % nz, core)).start()
        to, slot_of = onward(k)
        if k // each == sections - 1:

            @pl.when(section == sections - 1)
            def _():
                pltpu.make_async_copy(own, passed.at[slot_of], pass_r.at[slot_of]).start()

            @pl.when(section < sections - 1)
            def _():
                remote(own, passed.at[slot_of], pass_s.at[0], pass_r.at[slot_of], to, place).start()

        else:
            remote(own, passed.at[slot_of], pass_s.at[0], pass_r.at[slot_of], to, place).start()

    def gather_y(k, dp):
        p = (pair + dp) % pairs
        block = full.at[k, core, y, partner] if dp == 0 else full.at[k, core, y, pl.ds(2 * p, 2)]
        remote(block, block, gz_s.at[0], gz_r.at[k, p], section, sibling).wait_recv()
        block = full.at[k, core, y, pl.ds(2 * p, 2)]
        for d in far_y:
            remote(block, block, gy_s.at[0], gy_r.at[k, y], section, at((y + d) % ny, z, core)).start()

    def multiply(k, c, y_, first):
        squared = None
        scaled = []
        for z_ in range(nz):
            value = full[k, c, y_, z_].astype(f32)
            squared = value * value if squared is None else squared + value * value
            scaled.append((value * gain_p[c, y_, :, z_ * 128 : (z_ + 1) * 128]).astype(bf16))
        product = jnp.dot(jnp.concatenate(scaled, axis=1), both_w[c, y_], preferred_element_type=f32)
        if first:
            squares[k] = squared
            products[k] = product
        else:
            squares[k] += squared
            products[k] += product

    def to_core(k, d):
        other = (y + d) % ny
        block = full.at[k, core, other]
        if d:
            remote(block, block, gy_s.at[0], gy_r.at[k, other], section, sibling).wait_recv()
        remote(block, block, gc_s.at[0], gc_r.at[k, other], section, sibling).start()
        multiply(k, core, other, d == 0)

    def of_core(k, d):
        other = (y + d) % ny
        block = full.at[k, 1 - core, other]
        remote(block, block, gc_s.at[0], gc_r.at[k, other], section, sibling).wait_recv()
        multiply(k, 1 - core, other, False)

    def down(k, _):
        width = 2 * ny * depth
        scale = lax.rsqrt(jnp.sum(squares[k], axis=-1, keepdims=True) / width + 1e-06)
        gate = products[k, :, :hidden_units] * scale
        up = products[k, :, half : half + hidden_units] * scale
        hidden = (gate / (1.0 + jnp.exp(-gate)) * up).astype(bf16)
        for c in (1 - core, core):
            for d in far_y + [0]:
                other = (y + d) % ny
                value = jnp.dot(hidden, down_p[c, other], preferred_element_type=f32).astype(bf16)
                for z_ in range(nz):
                    parts[k, c, other, z_] = value[:, z_ * 128 : (z_ + 1) * 128]
                if c is not core:
                    remote(
                        parts.at[k, c, other],
                        from_core.at[k, other],
                        rc_s.at[0],
                        rc_r.at[k, other],
                        section,
                        sibling,
                    ).start()

    far_pairs = near_first(pairs)[::-1]

    def add_core(k, _):
        for d in far_y + [0]:
            other = (y + d) % ny
            remote(
                parts.at[k, 1 - core, other],
                from_core.at[k, other],
                rc_s.at[0],
                rc_r.at[k, other],
                section,
                sibling,
            ).wait_recv()
            by_core[k, other] = (parts[k, core, other].astype(f32) + from_core[k, other].astype(f32)).astype(bf16)
            if d:
                for dp in far_pairs:
                    p = (pair + dp) % pairs
                    remote(
                        by_core.at[k, other, pl.ds(2 * p, 2)],
                        from_y.at[k, p, d - 1],
                        ry_s.at[0],
                        ry_r.at[k, p],
                        section,
                        at(other, z, core),
                    ).start()

    def sum_y(k, dp):
        p = (pair + dp) % pairs
        block = from_y.at[k, p]
        remote(block, block, ry_s.at[0], ry_r.at[k, p], section, sibling).wait_recv()
        to, slot_of = onward(k)
        for other in (partner, z) if dp == 0 else (2 * p, 2 * p + 1):
            value = by_core[k, y, other].astype(f32)
            for d in range(1, ny):
                value = value + from_y[k, p, d - 1, other % 2].astype(f32)
            by_y[k, other] = value.astype(bf16)
            copy = remote(
                by_y.at[k, other], from_z.at[slot_of, z], rz_s.at[0], rz_r.at[slot_of], to, at(y, other, core)
            )
            if other is z and k // each == sections - 1:

                @pl.when(section == sections - 1)
                def _():
                    pltpu.make_async_copy(by_y.at[k, z], from_z.at[slot_of, z], rz_r.at[slot_of]).start()

                @pl.when(section < sections - 1)
                def _():
                    copy.start()

            else:
                copy.start()

    steps = [(begin, 0)]
    steps += [(gather_y, dp) for dp in near_first(pairs)]
    steps += [(to_core, d) for d in near_first(ny)]
    steps += [(of_core, d) for d in near_first(ny)]
    steps += [(down, 0), (add_core, 0)]
    steps += [(sum_y, dp) for dp in far_pairs]
    order = ORDER if len(ORDER) == chunks * len(steps) else tuple(range(chunks)) * len(steps)
    taken_steps = [0] * chunks
    for k in order:
        step, which_one = steps[taken_steps[k]]
        taken_steps[k] += 1
        step(k, which_one)

    def sent(block, sem):
        remote(block, block, sem, pass_r.at[0], section, sibling).wait_send()

    sent(small.at[pl.ds(0, nz - 1)], small_s.at[0])
    sent(audio.at[core, pl.ds(0, ny - 1)], audio_y_s.at[0])
    sent(audio.at[core], audio_c_s.at[0])
    sent(full.at[:, core, y, pl.ds(0, nz - 1)], gz_s.at[0])
    sent(full.at[:, core, pl.ds(0, ny - 1)], gy_s.at[0])
    sent(full.at[:, core], gc_s.at[0])
    sent(from_core.at[...], rc_s.at[0])
    sent(by_core.at[:, pl.ds(0, ny - 1)], ry_s.at[0])

    @pl.when(section < sections - 1)
    def _():
        sent(by_y.at[...], rz_s.at[0])
        sent(passed.at[pl.ds(0, chunks)], pass_s.at[0])

    @pl.when(section == sections - 1)
    def _():
        sent(by_y.at[pl.ds(0, chunks - each)], rz_s.at[0])
        sent(by_y.at[pl.ds(0, each), pl.ds(0, nz - 1)], rz_s.at[0])
        sent(passed.at[pl.ds(0, chunks - each)], pass_s.at[0])

    for i in range(each):
        wait_stream(chunks + i)
        out_ref[i * rows : (i + 1) * rows, :] = total_of(chunks + i)


def on_device(
    sections,
    ny,
    nz,
    enc_states,
    clip_frames,
    clip_offset,
    ln_gain,
    ln_bias,
    w_proj,
    proj_bias,
    text_embed,
    norm_gain,
    w_gate,
    w_up,
    w_down,
):
    tokens, micro, feat = text_embed.shape
    total = tokens * micro
    hidden_units, width = w_gate.shape[1:]
    chunks = CHUNKS
    rows = total // chunks
    each = chunks // sections
    enc_width = enc_states.shape[-1]
    small_rows = -(-2 * (enc_width // 128) // 8) * 8
    half = -(-hidden_units // 128) * 128
    bf16, f32 = jnp.bfloat16, jnp.float32
    hbm = pl.BlockSpec(memory_space=pl.ANY)
    dma = pltpu.SemaphoreType.DMA
    args = (
        enc_states,
        clip_frames.reshape(1, -1),
        clip_offset.reshape(1, -1),
        ln_gain.reshape(-1, 128),
        ln_bias.reshape(-1, 128),
        w_proj,
        proj_bias.reshape(1, -1),
        text_embed.reshape(total, feat),
        norm_gain,
        w_gate,
        w_up,
        w_down,
    )
    out = pl.pallas_call(
        functools.partial(kernel, sections, ny, nz),
        out_shape=jax.ShapeDtypeStruct((total // sections, feat), bf16),
        in_specs=[hbm] * len(args),
        out_specs=pl.BlockSpec(memory_space=pltpu.VMEM),
        scratch_shapes=[pltpu.VMEM(arg.shape, arg.dtype) for arg in args]
        + [
            pltpu.VMEM((2, ny, nz * feat, 2 * half), bf16),
            pltpu.VMEM((2, ny, hidden_units, nz * feat), bf16),
            pltpu.VMEM((2, ny, 1, nz * feat), f32),
            pltpu.VMEM((nz, small_rows, 128), f32),
            pltpu.VMEM((2, ny, 2 * nz, enc_width), bf16),
            pltpu.VMEM((total, feat), bf16),
            pltpu.VMEM((chunks, 2, ny, nz, rows, feat), bf16),
            pltpu.VMEM((chunks, rows, 2 * half), f32),
            pltpu.VMEM((chunks, rows, feat), f32),
            pltpu.VMEM((chunks, 2, ny, nz, rows, feat), bf16),
            pltpu.VMEM((chunks, ny, nz, rows, feat), bf16),
            pltpu.VMEM((chunks, ny, nz, rows, feat), bf16),
            pltpu.VMEM((chunks, nz // 2, ny - 1, 2, rows, feat), bf16),
            pltpu.VMEM((chunks, nz, rows, feat), bf16),
            pltpu.VMEM((chunks + each, nz, rows, feat), bf16),
            pltpu.VMEM((chunks + each, rows, feat), bf16),
            dma((len(args),)),
            dma((1,)),
            dma((1,)),
            dma((1,)),
            dma((ny,)),
            dma((1,)),
            dma((1,)),
            dma((1,)),
            dma((chunks, nz // 2)),
            dma((1,)),
            dma((chunks, ny)),
            dma((1,)),
            dma((chunks, ny)),
            dma((1,)),
            dma((chunks, ny)),
            dma((1,)),
            dma((chunks, nz // 2)),
            dma((1,)),
            dma((chunks + each,)),
            dma((1,)),
            dma((chunks + each,)),
        ],
        compiler_params=pltpu.CompilerParams(
            collective_id=0, has_side_effects=True, vmem_limit_bytes=62 * 2**20
        ),
        cost_estimate=pl.CostEstimate(
            flops=6 * total * hidden_units * width, bytes_accessed=6 * hidden_units * width, transcendentals=0
        ),
    )(*args)
    return out.reshape(tokens // sections, micro, feat)


def solution(mesh):
    sections, spread = mesh.shape["section"], mesh.shape["fsdp"]
    ny = 4 if spread == 64 else 2
    nz = spread // (2 * ny)
    placed = (
        P("fsdp", None, None),
        P(),
        P(),
        P(),
        P(),
        P(None, "fsdp"),
        P("fsdp"),
        P(None, None, "fsdp"),
        P("section", None),
        P("section", "fsdp", None),
        P("section", "fsdp", None),
        P("section", "fsdp", None),
    )
    return jax.shard_map(
        functools.partial(on_device, sections, ny, nz),
        mesh=mesh,
        in_specs=placed,
        out_specs=P("section", None, "fsdp"),
        check_vma=False,
    )
```

```python
import functools

import jax
import jax.numpy as jnp
from jax import lax
from jax.experimental import pallas as pl
from jax.experimental.pallas import tpu as pltpu
from jax.sharding import PartitionSpec as P

MESH = pl.DeviceIdType.MESH
CHUNKS = 4
ORDER = (
    0, 0, 0, 0, 0, 0, 1, 1, 0, 0, 1, 0, 1, 1, 0, 0, 0, 0, 2, 0, 1, 0, 1, 1, 2, 1, 1, 2, 2, 1, 3, 1, 1, 2, 1, 0, 0, 1,
    0, 0, 3, 3, 2, 3, 2, 2, 2, 3, 3, 2, 2, 2, 2, 2, 1, 1, 1, 2, 1, 3, 3, 3, 3, 3, 3, 3, 3, 2, 2, 3, 2, 2, 3, 3, 3, 3,
)


def near_first(count):
    return sorted(range(count), key=lambda d: (min(d, count - d), d))


def remote(src, dst, send, recv, section, place):
    return pltpu.make_async_remote_copy(
        src_ref=src,
        dst_ref=dst,
        send_sem=send,
        recv_sem=recv,
        device_id=(section, place),
        device_id_type=MESH,
    )


def kernel(
    sections,
    ny,
    nz,
    enc_hbm,
    frames_hbm,
    offset_hbm,
    ln_gain_hbm,
    ln_bias_hbm,
    proj_hbm,
    proj_bias_hbm,
    text_hbm,
    gain_hbm,
    gate_hbm,
    up_hbm,
    down_hbm,
    out_ref,
    enc_ref,
    frames_ref,
    offset_ref,
    ln_gain_ref,
    ln_bias_ref,
    proj_ref,
    proj_bias_ref,
    text_ref,
    gain_ref,
    gate_w,
    up_w,
    down_w,
    both_w,
    down_p,
    gain_p,
    small,
    audio,
    embedded,
    full,
    products,
    squares,
    parts,
    from_core,
    by_core,
    from_y,
    by_y,
    from_z,
    passed,
    load_sem,
    small_s,
    small_r,
    audio_y_s,
    audio_y_r,
    audio_c_s,
    audio_c_r,
    gz_s,
    gz_r,
    gy_s,
    gy_r,
    gc_s,
    gc_r,
    rc_s,
    rc_r,
    ry_s,
    ry_r,
    rz_s,
    rz_r,
    pass_s,
    pass_r,
):
    f32, bf16 = jnp.float32, jnp.bfloat16
    section = lax.axis_index("section")
    place = lax.axis_index("fsdp")
    core = place % 2
    z = (place // 2) % nz
    y = place // (2 * nz)
    pair = z // 2
    partner = 2 * pair + 1 - z % 2
    pairs = nz // 2
    chunks, rows = full.shape[0], full.shape[4]
    total = chunks * rows
    each = chunks // sections
    last = section // (sections - 1)
    enc_width = enc_ref.shape[-1]
    tiles = enc_width // 128
    hidden_units = gate_w.shape[1]
    half = both_w.shape[-1] // 2
    depth = nz * 128

    def at(y_, z_, core_):
        return (y_ * nz + z_) * 2 + core_

    sibling = at(y, z, 1 - core)

    loads = [
        pltpu.make_async_copy(src, dst, load_sem.at[i])
        for i, (src, dst) in enumerate(
            (
                (enc_hbm, enc_ref),
                (ln_gain_hbm, ln_gain_ref),
                (ln_bias_hbm, ln_bias_ref),
                (frames_hbm, frames_ref),
                (offset_hbm, offset_ref),
                (gain_hbm, gain_ref),
                (down_hbm, down_w),
                (gate_hbm, gate_w),
                (up_hbm, up_w),
                (proj_hbm, proj_ref),
                (proj_bias_hbm, proj_bias_ref),
                (text_hbm, text_ref),
            )
        )
    ]
    for load in loads[:3]:
        load.start()

    barrier = pltpu.get_barrier_semaphore()

    def greet(section_, places):
        for place_ in places:
            pl.semaphore_signal(barrier, inc=1, device_id=(section_, place_), device_id_type=MESH)
        return len(places)

    beside = [at(y, (z + d) % nz, core) for d in range(1, nz)]
    onwards = greet((section + sections - 1) % sections, [place] + beside)
    greeted = greet(section, beside + [at((y + d) % ny, z, core) for d in range(1, ny)] + [sibling])

    @pl.when((section > 0) & (section < sections - 1))
    def _():
        greet(sections - 1, [place] + beside)

    for load in loads[3:]:
        load.start()

    small[z] = jnp.zeros(small.shape[1:], f32)
    for load in loads[:3]:
        load.wait()
    frames = enc_ref[0].astype(f32)
    for j in range(2):
        pooled = 0.5 * (frames[2 * j : 2 * j + 1] + frames[2 * j + 1 : 2 * j + 2])
        centred = pooled - jnp.mean(pooled, axis=-1, keepdims=True)
        spread = jnp.mean(centred * centred, axis=-1, keepdims=True)
        normed = centred * lax.rsqrt(spread + 1e-05)
        for t in range(tiles):
            row = normed[:, t * 128 : (t + 1) * 128] * ln_gain_ref[t : t + 1] + ln_bias_ref[t : t + 1]
            small[z, j * tiles + t : j * tiles + t + 1, :] = row.astype(bf16).astype(f32)
    pl.semaphore_wait(barrier, greeted + onwards * (1 + (sections - 2) * last))

    far_z = near_first(nz)[:0:-1]
    far_y = near_first(ny)[:0:-1]
    for d in far_z:
        other = (z + d) % nz
        copy = remote(small.at[z], small.at[z], small_s.at[0], small_r.at[0], section, at(y, other, core))
        copy.start()

    for load in loads[3:8]:
        load.wait()
    clips = ny * nz * 2
    row_of = lax.broadcasted_iota(jnp.int32, (clips, 2 * clips), 1)
    clip_of = lax.broadcasted_iota(jnp.int32, (clips, 2 * clips), 0)
    holds = ((row_of // (2 * nz) % ny) * nz + row_of % nz) * 2 + row_of // (2 * nz * ny)
    which = row_of // nz % 2
    spots = jnp.zeros((8, 2 * clips), f32)
    for j in range(2):
        spot = offset_ref[...] + j
        tokens = total // 2
        target = jnp.where(2 * j < frames_ref[...], spot % tokens * 2 + spot // tokens, total)
        order = jnp.where((holds == clip_of) & (which == j), 1.0, 0.0).astype(bf16)
        spread_target = jnp.broadcast_to(target.astype(f32), (8, clips)).astype(bf16)
        spots = spots + jnp.dot(spread_target, order, preferred_element_type=f32)
    slot = lax.broadcasted_iota(jnp.int32, (total, 2 * clips), 0).astype(f32)
    chosen = jnp.where(slot == spots[0:1], 1.0, 0.0)
    taken = jnp.sum(chosen, axis=-1, keepdims=True)
    chosen = chosen.astype(bf16)

    def lanes_of(c, y_, z_):
        return pl.ds(pl.multiple_of(at(y_, z_, c) * 128, 128), 128)

    def arrange_gate(i, carry):
        c, y_ = i // ny, i % ny
        for z_ in range(nz):
            lanes = lanes_of(c, y_, z_)
            here = pl.ds(z_ * 128, 128)
            gain_p[c, y_, :, here] = gain_ref[:, lanes]
            down_p[c, y_, :, here] = down_w[0, :, lanes]
            both_w[c, y_, here, half - 128 : half] = jnp.zeros((128, 128), bf16)
            both_w[c, y_, here, :hidden_units] = gate_w[0, :, lanes].T
        return carry

    def arrange_up(i, carry):
        c, y_ = i // ny, i % ny
        for z_ in range(nz):
            here = pl.ds(z_ * 128, 128)
            both_w[c, y_, here, 2 * half - 128 :] = jnp.zeros((128, 128), bf16)
            both_w[c, y_, here, half : half + hidden_units] = up_w[0, :, lanes_of(c, y_, z_)].T
        return carry

    lax.fori_loop(0, 2 * ny, arrange_gate, 0)

    block = small.at[pl.ds(0, nz - 1)]
    remote(block, block, small_s.at[0], small_r.at[0], section, sibling).wait_recv()
    for t in range(tiles):
        two = jnp.concatenate([small[:, t, :], small[:, tiles + t, :]], axis=0)
        audio[core, y, :, t * 128 : (t + 1) * 128] = two.astype(bf16)
    for d in far_y:
        block = audio.at[core, y]
        remote(block, block, audio_y_s.at[0], audio_y_r.at[y], section, at((y + d) % ny, z, core)).start()
    remote(block, block, audio_c_s.at[0], audio_c_r.at[0], section, sibling).start()
    for load in loads[8:]:
        load.wait()
    lax.fori_loop(0, 2 * ny, arrange_up, 0)
    for d in far_y[::-1]:
        other = (y + d) % ny
        block = audio.at[core, other]
        remote(block, block, audio_y_s.at[0], audio_y_r.at[other], section, sibling).wait_recv()
        remote(block, block, audio_c_s.at[0], audio_c_r.at[0], section, sibling).start()
    block = audio.at[1 - core]
    remote(block, block, audio_c_s.at[0], audio_c_r.at[0], section, sibling).wait_recv()
    gathered = audio[...].reshape(2 * clips, enc_width)
    projected = jnp.dot(gathered, proj_ref[...], preferred_element_type=f32) + proj_bias_ref[...]
    placed = jnp.dot(chosen, projected.astype(bf16), preferred_element_type=f32)
    embedded[...] = jnp.where(taken > 0.0, placed, text_ref[...].astype(f32)).astype(bf16)

    def total_of(k):
        value = passed[k].astype(f32)
        for other in range(nz):
            value = value + from_z[k, other].astype(f32)
        return value.astype(bf16)

    def wait_stream(k):
        remote(from_z.at[k], from_z.at[k], rz_s.at[0], rz_r.at[k], section, sibling).wait_recv()
        remote(passed.at[k], passed.at[k], pass_s.at[0], pass_r.at[k], section, sibling).wait_recv()

    def onward(k):
        to = (section + 1) * (1 - last) + (k // each) * last
        slot_of = k + last * (chunks + k % each - k)
        return to, slot_of

    def begin(k, _):
        own = full.at[k, core, y, z]

        @pl.when(section == 0)
        def _():
            own[...] = embedded[k * rows : (k + 1) * rows, :]

        @pl.when(section > 0)
        def _():
            wait_stream(k)
            own[...] = total_of(k)

        for d in far_z:
            remote(own, own, gz_s.at[0], gz_r.at[k, pair], section, at(y, (z + d) % nz, core)).start()
        to, slot_of = onward(k)
        if k // each == sections - 1:

            @pl.when(section == sections - 1)
            def _():
                pltpu.make_async_copy(own, passed.at[slot_of], pass_r.at[slot_of]).start()

            @pl.when(section < sections - 1)
            def _():
                remote(own, passed.at[slot_of], pass_s.at[0], pass_r.at[slot_of], to, place).start()

        else:
            remote(own, passed.at[slot_of], pass_s.at[0], pass_r.at[slot_of], to, place).start()

    def gather_y(k, dp):
        p = (pair + dp) % pairs
        block = full.at[k, core, y, partner] if dp == 0 else full.at[k, core, y, pl.ds(2 * p, 2)]
        remote(block, block, gz_s.at[0], gz_r.at[k, p], section, sibling).wait_recv()
        block = full.at[k, core, y, pl.ds(2 * p, 2)]
        for d in far_y:
            remote(block, block, gy_s.at[0], gy_r.at[k, y], section, at((y + d) % ny, z, core)).start()

    def multiply(k, c, y_, first):
        squared = None
        scaled = []
        for z_ in range(nz):
            value = full[k, c, y_, z_].astype(f32)
            squared = value * value if squared is None else squared + value * value
            scaled.append((value * gain_p[c, y_, :, z_ * 128 : (z_ + 1) * 128]).astype(bf16))
        product = jnp.dot(jnp.concatenate(scaled, axis=1), both_w[c, y_], preferred_element_type=f32)
        if first:
            squares[k] = squared
            products[k] = product
        else:
            squares[k] += squared
            products[k] += product

    def to_core(k, d):
        other = (y + d) % ny
        block = full.at[k, core, other]
        if d:
            remote(block, block, gy_s.at[0], gy_r.at[k, other], section, sibling).wait_recv()
        remote(block, block, gc_s.at[0], gc_r.at[k, other], section, sibling).start()
        multiply(k, core, other, d == 0)

    def of_core(k, d):
        other = (y + d) % ny
        block = full.at[k, 1 - core, other]
        remote(block, block, gc_s.at[0], gc_r.at[k, other], section, sibling).wait_recv()
        multiply(k, 1 - core, other, False)

    def down(k, _):
        width = 2 * ny * depth
        scale = lax.rsqrt(jnp.sum(squares[k], axis=-1, keepdims=True) / width + 1e-06)
        gate = products[k, :, :hidden_units] * scale
        up = products[k, :, half : half + hidden_units] * scale
        hidden = (gate / (1.0 + jnp.exp(-gate)) * up).astype(bf16)
        for c in (1 - core, core):
            for d in far_y + [0]:
                other = (y + d) % ny
                value = jnp.dot(hidden, down_p[c, other], preferred_element_type=f32).astype(bf16)
                for z_ in range(nz):
                    parts[k, c, other, z_] = value[:, z_ * 128 : (z_ + 1) * 128]
                if c is not core:
                    remote(
                        parts.at[k, c, other],
                        from_core.at[k, other],
                        rc_s.at[0],
                        rc_r.at[k, other],
                        section,
                        sibling,
                    ).start()

    far_pairs = near_first(pairs)[::-1]

    def add_core(k, _):
        for d in far_y + [0]:
            other = (y + d) % ny
            remote(
                parts.at[k, 1 - core, other],
                from_core.at[k, other],
                rc_s.at[0],
                rc_r.at[k, other],
                section,
                sibling,
            ).wait_recv()
            by_core[k, other] = (parts[k, core, other].astype(f32) + from_core[k, other].astype(f32)).astype(bf16)
            if d:
                for dp in far_pairs:
                    p = (pair + dp) % pairs
                    remote(
                        by_core.at[k, other, pl.ds(2 * p, 2)],
                        from_y.at[k, p, d - 1],
                        ry_s.at[0],
                        ry_r.at[k, p],
                        section,
                        at(other, z, core),
                    ).start()

    def sum_y(k, dp):
        p = (pair + dp) % pairs
        block = from_y.at[k, p]
        remote(block, block, ry_s.at[0], ry_r.at[k, p], section, sibling).wait_recv()
        to, slot_of = onward(k)
        for other in (partner, z) if dp == 0 else (2 * p, 2 * p + 1):
            value = by_core[k, y, other].astype(f32)
            for d in range(1, ny):
                value = value + from_y[k, p, d - 1, other % 2].astype(f32)
            by_y[k, other] = value.astype(bf16)
            copy = remote(
                by_y.at[k, other], from_z.at[slot_of, z], rz_s.at[0], rz_r.at[slot_of], to, at(y, other, core)
            )
            if other is z and k // each == sections - 1:

                @pl.when(section == sections - 1)
                def _():
                    pltpu.make_async_copy(by_y.at[k, z], from_z.at[slot_of, z], rz_r.at[slot_of]).start()

                @pl.when(section < sections - 1)
                def _():
                    copy.start()

            else:
                copy.start()

    steps = [(begin, 0)]
    steps += [(gather_y, dp) for dp in near_first(pairs)]
    steps += [(to_core, d) for d in near_first(ny)]
    steps += [(of_core, d) for d in near_first(ny)]
    steps += [(down, 0), (add_core, 0)]
    steps += [(sum_y, dp) for dp in far_pairs]
    order = ORDER if len(ORDER) == chunks * len(steps) else tuple(range(chunks)) * len(steps)
    taken_steps = [0] * chunks
    for k in order:
        step, which_one = steps[taken_steps[k]]
        taken_steps[k] += 1
        step(k, which_one)

    def sent(block, sem):
        remote(block, block, sem, pass_r.at[0], section, sibling).wait_send()

    sent(small.at[pl.ds(0, nz - 1)], small_s.at[0])
    sent(audio.at[core, pl.ds(0, ny - 1)], audio_y_s.at[0])
    sent(audio.at[core], audio_c_s.at[0])
    sent(full.at[:, core, y, pl.ds(0, nz - 1)], gz_s.at[0])
    sent(full.at[:, core, pl.ds(0, ny - 1)], gy_s.at[0])
    sent(full.at[:, core], gc_s.at[0])
    sent(from_core.at[...], rc_s.at[0])
    sent(by_core.at[:, pl.ds(0, ny - 1)], ry_s.at[0])

    @pl.when(section < sections - 1)
    def _():
        sent(by_y.at[...], rz_s.at[0])
        sent(passed.at[pl.ds(0, chunks)], pass_s.at[0])

    @pl.when(section == sections - 1)
    def _():
        sent(by_y.at[pl.ds(0, chunks - each)], rz_s.at[0])
        sent(by_y.at[pl.ds(0, each), pl.ds(0, nz - 1)], rz_s.at[0])
        sent(passed.at[pl.ds(0, chunks - each)], pass_s.at[0])

    for i in range(each):
        wait_stream(chunks + i)
        out_ref[i * rows : (i + 1) * rows, :] = total_of(chunks + i)


def on_device(
    sections,
    ny,
    nz,
    enc_states,
    clip_frames,
    clip_offset,
    ln_gain,
    ln_bias,
    w_proj,
    proj_bias,
    text_embed,
    norm_gain,
    w_gate,
    w_up,
    w_down,
):
    tokens, micro, feat = text_embed.shape
    total = tokens * micro
    hidden_units, width = w_gate.shape[1:]
    chunks = CHUNKS
    rows = total // chunks
    each = chunks // sections
    enc_width = enc_states.shape[-1]
    small_rows = -(-2 * (enc_width // 128) // 8) * 8
    half = -(-hidden_units // 128) * 128
    bf16, f32 = jnp.bfloat16, jnp.float32
    hbm = pl.BlockSpec(memory_space=pl.ANY)
    dma = pltpu.SemaphoreType.DMA
    args = (
        enc_states,
        clip_frames.reshape(1, -1),
        clip_offset.reshape(1, -1),
        ln_gain.reshape(-1, 128),
        ln_bias.reshape(-1, 128),
        w_proj,
        proj_bias.reshape(1, -1),
        text_embed.reshape(total, feat),
        norm_gain,
        w_gate,
        w_up,
        w_down,
    )
    out = pl.pallas_call(
        functools.partial(kernel, sections, ny, nz),
        out_shape=jax.ShapeDtypeStruct((total // sections, feat), bf16),
        in_specs=[hbm] * len(args),
        out_specs=pl.BlockSpec(memory_space=pltpu.VMEM),
        scratch_shapes=[pltpu.VMEM(arg.shape, arg.dtype) for arg in args]
        + [
            pltpu.VMEM((2, ny, nz * feat, 2 * half), bf16),
            pltpu.VMEM((2, ny, hidden_units, nz * feat), bf16),
            pltpu.VMEM((2, ny, 1, nz * feat), f32),
            pltpu.VMEM((nz, small_rows, 128), f32),
            pltpu.VMEM((2, ny, 2 * nz, enc_width), bf16),
            pltpu.VMEM((total, feat), bf16),
            pltpu.VMEM((chunks, 2, ny, nz, rows, feat), bf16),
            pltpu.VMEM((chunks, rows, 2 * half), f32),
            pltpu.VMEM((chunks, rows, feat), f32),
            pltpu.VMEM((chunks, 2, ny, nz, rows, feat), bf16),
            pltpu.VMEM((chunks, ny, nz, rows, feat), bf16),
            pltpu.VMEM((chunks, ny, nz, rows, feat), bf16),
            pltpu.VMEM((chunks, nz // 2, ny - 1, 2, rows, feat), bf16),
            pltpu.VMEM((chunks, nz, rows, feat), bf16),
            pltpu.VMEM((chunks + each, nz, rows, feat), bf16),
            pltpu.VMEM((chunks + each, rows, feat), bf16),
            dma((len(args),)),
            dma((1,)),
            dma((1,)),
            dma((1,)),
            dma((ny,)),
            dma((1,)),
            dma((1,)),
            dma((1,)),
            dma((chunks, nz // 2)),
            dma((1,)),
            dma((chunks, ny)),
            dma((1,)),
            dma((chunks, ny)),
            dma((1,)),
            dma((chunks, ny)),
            dma((1,)),
            dma((chunks, nz // 2)),
            dma((1,)),
            dma((chunks + each,)),
            dma((1,)),
            dma((chunks + each,)),
        ],
        compiler_params=pltpu.CompilerParams(
            collective_id=0, has_side_effects=True, vmem_limit_bytes=62 * 2**20
        ),
        cost_estimate=pl.CostEstimate(
            flops=6 * total * hidden_units * width, bytes_accessed=6 * hidden_units * width, transcendentals=0
        ),
    )(*args)
    return out.reshape(tokens // sections, micro, feat)


def solution(mesh):
    sections, spread = mesh.shape["section"], mesh.shape["fsdp"]
    ny = 4 if spread == 64 else 2
    nz = spread // (2 * ny)
    placed = (
        P("fsdp", None, None),
        P(),
        P(),
        P(),
        P(),
        P(None, "fsdp"),
        P("fsdp"),
        P(None, None, "fsdp"),
        P("section", None),
        P("section", "fsdp", None),
        P("section", "fsdp", None),
        P("section", "fsdp", None),
    )
    return jax.shard_map(
        functools.partial(on_device, sections, ny, nz),
        mesh=mesh,
        in_specs=placed,
        out_specs=P("section", None, "fsdp"),
        check_vma=False,
    )
```
